128 devices in a mesh: row: 16 (over x_lo, y, core), col: 8 (over z, x_hi).
Axes of the slice: x: 4 (x_hi: 2, x_lo: 2; x = x_hi * 2 + x_lo), y: 4, z: 4, core: 2. Of those that a mesh axis runs over, the one named last changes fastest.
Arguments:
- pair: bfloat16 [512, 512, 128], P('row', 'col'), may hold values from -6 to 6
- mask: int32 [512], replicated, may hold values 0 or 1
- tri_in: bfloat16 [128, 640], replicated, may hold values from -0.5 to 0.5
- tri_out: bfloat16 [128, 128], replicated, may hold values from -0.5 to 0.5
- start_in: bfloat16 [128, 512], replicated, may hold values from -0.5 to 0.5
- start_bias: bfloat16 [128, 4], replicated, may hold values from -30 to 30
- start_out: bfloat16 [128, 128], replicated, may hold values from -0.5 to 0.5
- end_in: bfloat16 [128, 512], replicated, may hold values from -0.5 to 0.5
- end_bias: bfloat16 [128, 4], replicated, may hold values from -30 to 30
- end_out: bfloat16 [128, 128], replicated, may hold values from -0.5 to 0.5
Outputs:
- pair_out: bfloat16 [512, 512, 128], P('row', 'col')
The draws below stay inside these ranges and needn't reach their ends.
All inputs are finite; a program needn't handle non-finite values.
Results may differ from the reference program's by a relative error of at most 0.035.
The reference program's roundings to bfloat16 on the way count: a program that leaves them out, or rounds other values in their place, can miss the bound.
Values may be sent and summed in bfloat16 or wider, within the bound.
No kernel may reach another device: no remote copies, remote signals or barrier semaphores. Data moves between devices by JAX's collectives and lax.ppermute only.
A program may use at most 128 MiB of HBM per device.

```python
import math
import jax
import jax.numpy as jnp
from jax import lax

C = 128
H = 4
D = 32
N = 512


def bias_weights(key, spread):
    return jnp.clip(spread * jax.random.normal(key, (C, H), jnp.float32), -30.0, 30.0).astype(jnp.bfloat16)


def draw_start_bias(key, part):
    key = jax.random.fold_in(key, 5)
    spread = 1.5 / math.sqrt(C)
    return bias_weights(key, spread)


def draw_end_bias(key, part):
    key = jax.random.fold_in(key, 9)
    spread = 1.5 / math.sqrt(C)
    return bias_weights(key, spread)


def set_ends(drawn, key, least, largest):
    spot = [jax.random.randint(jax.random.fold_in(key, axis), (), 0, length) for axis, length in enumerate(drawn.shape)]
    main_axis = drawn.shape.index(max(drawn.shape))
    beside = spot[:main_axis] + [(spot[main_axis] + 1) % drawn.shape[main_axis]] + spot[main_axis + 1:]
    return drawn.at[tuple(spot)].set(least).at[tuple(beside)].set(largest)


def block_levels(key, extent, pieces, least, largest):
    level = 1.0
    for axis_at, shards_of in pieces:
        steps = jax.random.uniform(jax.random.fold_in(jax.random.fold_in(key, 6), axis_at), (shards_of,), jnp.float32, least / len(pieces), largest / len(pieces))
        level = level * jnp.repeat(jnp.exp(steps), extent[axis_at] // shards_of).reshape((-1,) + (1,) * (len(extent) - 1 - axis_at))
    return level


def bell_draw(key, shape, scale, most, split=(), kind=jnp.bfloat16):
    result = jax.random.normal(key, shape, jnp.float32) * scale
    if len(split) > 0:
        result = block_levels(key, shape, split, -0.22, 0.18) * result
    return jnp.clip(result, min=-most, max=most).astype(kind)


def setup_inputs(seed: int = 0) -> dict:
    key_list = jax.random.split(jax.random.key(seed), 11)
    return {
        "pair": bell_draw(key_list[0], (N, N, C), 1.0, 6.0, ((0, 16), (1, 8))),
        "mask": set_ends((jax.random.randint(key_list[1], (N,), 0, 8) < 7).astype(jnp.int32), jax.random.fold_in(key_list[1], 1), 0, 1),
        "tri_in": bell_draw(key_list[2], (C, 5 * C), C ** -0.5, 0.5),
        "tri_out": bell_draw(key_list[3], (C, C), C ** -0.5, 0.5),
        "start_in": bell_draw(key_list[4], (C, 4 * C), C ** -0.5, 0.5),
        "start_bias": draw_start_bias(jax.random.fold_in(key_list[10], 71), 0),
        "start_out": bell_draw(key_list[6], (C, C), C ** -0.5, 0.5),
        "end_in": bell_draw(key_list[7], (C, 4 * C), C ** -0.5, 0.5),
        "end_bias": draw_end_bias(jax.random.fold_in(key_list[10], 71), 0),
        "end_out": bell_draw(key_list[9], (C, C), C ** -0.5, 0.5),
    }


epsilon = 1e-05

def layer_norm(values_in):
    average = lax.optimization_barrier(jnp.mean(values_in, axis=-1, keepdims=True))
    centred = values_in - average
    variance = lax.optimization_barrier(jnp.mean(centred * centred, axis=-1, keepdims=True))
    return centred * lax.rsqrt(variance + epsilon)

def attend_rows(pair_now, weights_in, weights_bias, weights_out, mask_float):
    pair_float = pair_now.astype(jnp.float32)
    normed = layer_norm(pair_float).astype(jnp.bfloat16)
    flat_rows = normed.reshape(N * N, C)
    projected = jnp.dot(flat_rows, weights_in, preferred_element_type=jnp.float32).reshape(N, N, 4 * C)
    query_heads = (projected[..., :C] * D ** (-0.5)).astype(jnp.bfloat16)
    key_heads = projected[..., C:2 * C].astype(jnp.bfloat16)
    value_heads = projected[..., 2 * C:3 * C].astype(jnp.bfloat16)
    query_heads, key_heads, value_heads = lax.optimization_barrier((query_heads, key_heads, value_heads))
    query_heads = query_heads.reshape(N, N, H, D)
    key_heads = key_heads.reshape(N, N, H, D)
    value_heads = value_heads.reshape(N, N, H, D)
    gating = jax.nn.sigmoid(projected[..., 3 * C:])
    bias_terms = jnp.dot(flat_rows, weights_bias, preferred_element_type=jnp.float32).reshape(N, N, H).transpose(2, 0, 1)
    mask_bias = (mask_float - 1.0) * 1000000000.0

    def one_row(row_items):
        row_query, row_keys, row_values = row_items
        scores = jnp.einsum('jhd,khd->hjk', row_query.astype(jnp.float32), row_keys.astype(jnp.float32))
        scores = scores + bias_terms + mask_bias
        weights = jax.nn.softmax(scores, axis=-1).astype(jnp.bfloat16)
        weights = lax.optimization_barrier(weights)
        return jnp.einsum('hjk,khd->jhd', weights.astype(jnp.float32), row_values.astype(jnp.float32)).reshape(N, C)
    attended = lax.map(one_row, (query_heads, key_heads, value_heads))
    gated_out = (attended * gating).astype(jnp.bfloat16)
    update = jnp.dot(gated_out.reshape(N * N, C), weights_out, preferred_element_type=jnp.float32).reshape(N, N, C)
    return (pair_float + update).astype(jnp.bfloat16)

def reference(pair, mask, tri_in, tri_out, start_in, start_bias, start_out, end_in, end_bias, end_out):
    mask_float = mask.astype(jnp.float32)
    pair_float = pair.astype(jnp.float32)
    normed = layer_norm(pair_float).astype(jnp.bfloat16)
    projected = jnp.dot(normed.reshape(N * N, C), tri_in, preferred_element_type=jnp.float32).reshape(N, N, 5 * C)
    pair_mask = mask_float[:, None, None] * mask_float[None, :, None]
    left_terms = (jax.nn.sigmoid(projected[..., :C]) * projected[..., C:2 * C] * pair_mask).astype(jnp.bfloat16)
    right_terms = (jax.nn.sigmoid(projected[..., 2 * C:3 * C]) * projected[..., 3 * C:4 * C] * pair_mask).astype(jnp.bfloat16)
    gating = jax.nn.sigmoid(projected[..., 4 * C:])
    left_terms, right_terms = lax.optimization_barrier((left_terms, right_terms))
    combined = jnp.einsum('ikc,jkc->ijc', left_terms.astype(jnp.float32), right_terms.astype(jnp.float32))
    mixed_norm = layer_norm(combined).astype(jnp.bfloat16)
    update = jnp.dot(mixed_norm.reshape(N * N, C), tri_out, preferred_element_type=jnp.float32).reshape(N, N, C)
    pair_one = (pair_float + gating * update).astype(jnp.bfloat16)
    pair_two = attend_rows(pair_one, start_in, start_bias, start_out, mask_float)
    pair_three = attend_rows(pair_two.transpose(1, 0, 2), end_in, end_bias, end_out, mask_float)
    return pair_three.transpose(1, 0, 2)
```

```python
import jax
import jax.numpy as jnp
from jax import lax
from jax.sharding import Mesh, PartitionSpec as P

everyone = ("xl", "y", "core", "z", "xh")
same_q = ("core", "z", "xh")
same_c = ("xl", "y", "core")
epsilon = 1e-05
bf16, f32 = jnp.bfloat16, jnp.float32


def swap(pieces, axes):
    return lax.all_to_all(pieces, axes, 0, 0, tiled=True)


def layer_norm(values_in, axis=-1):
    average = jnp.mean(values_in, axis=axis, keepdims=True)
    centred = values_in - average
    variance = jnp.mean(centred * centred, axis=axis, keepdims=True)
    return centred * lax.rsqrt(variance + epsilon)


def dot(a, b, dims):
    return lax.dot_general(a, b, (dims, ((), ())), preferred_element_type=f32)


def split_bias(bias, kept, axis):
    masked = jnp.where(kept, bias, -3e38)
    top = jnp.max(masked, axis=axis, keepdims=True)
    top = jnp.where(top > -1e38, top, jnp.max(bias, axis=axis, keepdims=True)).astype(bf16)
    rest = (bias - top.astype(f32)).astype(bf16)
    return top, rest


def attend(query, keys, values, bias, scores_spec):
    scores = jnp.einsum(scores_spec, query, keys, preferred_element_type=f32)
    return scores


def body(pair, mask, tri_in, tri_out, start_in, start_bias, start_out, end_in, end_bias, end_out):
    q = lax.axis_index(("xl", "y"))
    core = lax.axis_index("core")
    c = lax.axis_index(("z", "xh"))
    maskf = mask.astype(f32)
    mask_bias = (maskf - 1.0) * 1000000000.0

    pieces = pair.reshape(4, 8, 2, 32, 128).transpose(2, 1, 0, 3, 4).reshape(16, 128, 128)
    pair_rows = swap(pieces, same_q).reshape(2, 8, 4, 32, 128).transpose(0, 2, 1, 3, 4).reshape(2048, 128)

    normed = layer_norm(pair.astype(f32)).astype(bf16).reshape(2048, 128)
    terms = dot(tri_in[:, :512], normed, ((0,), (1,)))
    row_mask = lax.dynamic_slice_in_dim(maskf, (2 * q + core) * 32, 32)
    col_mask = lax.dynamic_slice_in_dim(maskf, c * 64, 64)
    pair_mask = (row_mask[:, None] * col_mask[None, :]).reshape(1, 2048)
    left = (jax.nn.sigmoid(terms[:128]) * terms[128:256] * pair_mask).astype(bf16)
    right = (jax.nn.sigmoid(terms[256:384]) * terms[384:512] * pair_mask).astype(bf16)
    both = jnp.concatenate([left.reshape(128, 16, 128), right.reshape(128, 16, 128)], axis=1)
    both = swap(both, everyone).reshape(16, 8, 2, 32, 64).transpose(2, 0, 3, 1, 4).reshape(2, 512, 512)
    combined = dot(both[0], both[1], ((1,), (1,))).astype(bf16)
    pieces = combined.reshape(8, 2, 4, 8, 8, 2, 32).transpose(0, 5, 3, 1, 2, 4, 6).reshape(128, 16, 128)
    combined = swap(pieces, everyone).reshape(128, 2048).astype(f32)

    mixed = layer_norm(combined, 0).astype(bf16)
    update = dot(mixed, tri_out, ((0,), (0,)))
    normed_rows = layer_norm(pair_rows.astype(f32)).astype(bf16)
    gate = jax.nn.sigmoid(dot(normed_rows, tri_in[:, 512:], ((1,), (0,))))
    pair_one = (pair_rows.astype(f32) + gate * update).astype(bf16)

    normed = layer_norm(pair_one.astype(f32)).astype(bf16)
    other = swap(jnp.broadcast_to(normed[None], (2, 2048, 128)), "core")
    normed_full = other.reshape(2, 8, 8, 32, 128).transpose(1, 2, 0, 3, 4).reshape(4096, 128)
    kept = lax.dynamic_index_in_dim(mask.reshape(8, 2, 32), core, 1, False).reshape(256) > 0
    bias = dot(start_bias, normed, ((0,), (1,))).reshape(4, 8, 256)
    top, rest = split_bias(bias, kept, 2)
    rest = rest.reshape(4, 2, 4, 256).transpose(1, 0, 2, 3).reshape(2, 32, 128)
    top = top.reshape(4, 2, 4).transpose(1, 0, 2).reshape(2, 1, 16)
    top = jnp.pad(top, ((0, 0), (0, 7), (0, 112)))
    pieces = jnp.concatenate([rest, top], axis=1)
    pieces = jnp.broadcast_to(pieces[None, :, None], (8, 2, 8, 40, 128)).reshape(128, 40, 128)
    pieces = swap(pieces, everyone)
    rest = pieces[:, :32].reshape(8, 2, 8, 4, 4, 8, 32).astype(f32)
    top = pieces[:, 32, :16].reshape(8, 2, 8, 4, 4, 1, 1).astype(f32)
    bias = (rest + top).transpose(3, 0, 4, 2, 5, 1, 6).reshape(4, 256, 512) + mask_bias
    scale = 32 ** (-0.5)
    query = (dot(normed, start_in[:, :128], ((1,), (0,))) * scale).astype(bf16).reshape(8, 256, 4, 32)
    keys = dot(normed_full, start_in[:, 128:256], ((1,), (0,))).astype(bf16).reshape(8, 512, 4, 32)
    values = dot(normed_full, start_in[:, 256:384], ((1,), (0,))).astype(bf16).reshape(8, 512, 4, 32)
    gate = jax.nn.sigmoid(dot(normed, start_in[:, 384:], ((1,), (0,))))
    scores = jnp.einsum("iqhd,ikhd->ihqk", query, keys, preferred_element_type=f32) + bias[None]
    weights = jax.nn.softmax(scores, axis=-1).astype(bf16)
    attended = jnp.einsum("ihqk,ikhd->iqhd", weights, values, preferred_element_type=f32)
    attended = (attended.reshape(2048, 128) * gate).astype(bf16)
    pair_two = (pair_one.astype(f32) + dot(attended, start_out, ((1,), (0,)))).astype(bf16)

    normed = layer_norm(pair_two.astype(f32)).astype(bf16)
    bias = dot(end_bias, normed, ((0,), (1,))).reshape(4, 8, 256)
    own = lax.dynamic_index_in_dim(mask.reshape(8, 2, 4, 8), c, 3, False)
    kept = lax.dynamic_index_in_dim(own, q, 0, False).reshape(8, 1) > 0
    top, rest = split_bias(bias, kept, 1)
    rest = rest.reshape(4, 8, 8, 2, 16).transpose(3, 0, 1, 2, 4).reshape(2, 32, 128)
    top = top.reshape(4, 8, 2, 16).transpose(2, 0, 1, 3).reshape(2, 4, 128)
    extra = jnp.concatenate([rest, jnp.pad(top, ((0, 0), (0, 4), (0, 0)))], axis=1)
    extra = jnp.broadcast_to(extra[None, :, None], (8, 2, 8, 40, 128)).reshape(128, 40, 128)
    pieces = pair_two.reshape(2, 2, 2, 8, 4, 8, 128).transpose(5, 1, 3, 4, 0, 2, 6).reshape(128, 16, 128)
    pieces = swap(jnp.concatenate([pieces, extra], axis=1), everyone)
    pair_two = pieces[:, :16].reshape(8, 2, 8, 4, 2, 2, 128).transpose(1, 3, 0, 4, 5, 2, 6).reshape(2048, 128)
    rest = pieces[:, 16:48].reshape(8, 2, 8, 4, 2, 4, 8, 16).astype(f32)
    top = pieces[:, 48:52].reshape(8, 2, 8, 4, 1, 1, 8, 16).astype(f32)
    bias = (rest + top).transpose(3, 0, 4, 5, 2, 6, 1, 7).reshape(4, 512, 256) + mask_bias[:, None]

    normed = layer_norm(pair_two.astype(f32)).astype(bf16)
    other = swap(jnp.broadcast_to(normed[None], (2, 2048, 128)), "core")
    normed_full = other.reshape(2, 8, 16, 16, 128).transpose(1, 2, 0, 3, 4).reshape(4096, 128)
    query = (dot(normed, end_in[:, :128], ((1,), (0,))) * scale).astype(bf16).reshape(8, 256, 4, 32)
    keys = dot(normed_full, end_in[:, 128:256], ((1,), (0,))).astype(bf16).reshape(8, 512, 4, 32)
    values = dot(normed_full, end_in[:, 256:384], ((1,), (0,))).astype(bf16).reshape(8, 512, 4, 32)
    gate = jax.nn.sigmoid(dot(normed, end_in[:, 384:], ((1,), (0,))))
    scores = jnp.einsum("ikhd,iqhd->ihkq", keys, query, preferred_element_type=f32) + bias[None]
    weights = jax.nn.softmax(scores, axis=2).astype(bf16)
    attended = jnp.einsum("ihkq,ikhd->iqhd", weights, values, preferred_element_type=f32)
    attended = (attended.reshape(2048, 128) * gate).astype(bf16)
    result = (pair_two.astype(f32) + dot(attended, end_out, ((1,), (0,)))).astype(bf16)

    pieces = result.reshape(8, 16, 16, 128).transpose(1, 2, 0, 3).reshape(16, 128, 128)
    pieces = swap(pieces, same_c).reshape(8, 2, 16, 8, 128).transpose(1, 2, 3, 0, 4)
    return pieces.reshape(32, 64, 128)


def solution(mesh):
    parts = Mesh(mesh.devices.reshape(2, 4, 2, 4, 2), everyone)
    placed = P(("xl", "y", "core"), ("z", "xh"), None)
    in_specs = (placed,) + (P(),) * 9
    return jax.shard_map(body, mesh=parts, in_specs=in_specs, out_specs=placed, check_vma=False)
```

```python
import jax
import jax.numpy as jnp
from jax import lax
from jax.experimental import pallas as pl
from jax.experimental.pallas import tpu as pltpu
from jax.sharding import Mesh, PartitionSpec as P

everyone = ("xl", "y", "core", "z", "xh")
same_q = ("core", "z", "xh")
same_c = ("xl", "y", "core")
epsilon = 1e-05
bf16, f32 = jnp.bfloat16, jnp.float32
log2e = 1.4426950408889634
lowest = -3e38


def swap(pieces, axes):
    return lax.all_to_all(pieces, axes, 0, 0, tiled=True)


def layer_norm(values_in, axis=-1):
    average = jnp.mean(values_in, axis=axis, keepdims=True)
    centred = values_in - average
    variance = jnp.mean(centred * centred, axis=axis, keepdims=True)
    return centred * lax.rsqrt(variance + epsilon)


def dot(a, b, dims):
    return lax.dot_general(a, b, (dims, ((), ())), preferred_element_type=f32)


def nn(a, b):
    return dot(a, b, ((1,), (0,)))


def nt(a, b):
    return dot(a, b, ((1,), (1,)))


def head_lanes(rows):
    lanes = lax.broadcasted_iota(jnp.int32, (rows, 128), 1)
    return [(lanes >= 32 * head) & (lanes < 32 * head + 32) for head in range(4)]


def start_kernel(core_ref, kept_ref, own_ref, other_ref, rest_ref, mask_ref, w_in_ref, w_out_ref, pair_ref, next_ref,
                 out_ref, extra_ref, bias_ref, after_ref):
    core = core_ref[0]
    to = lax.broadcasted_iota(jnp.int32, (256, 256), 0)
    place = (to // 16 % 2 * 8 + to % 8) * 16 + (to // 32 % 2 * 2 + to // 8 % 2) * 4 + to // 64
    order = (lax.broadcasted_iota(jnp.int32, (256, 256), 1) == place).astype(f32).astype(bf16)
    for half in range(2):
        source = core if half == 0 else 1 - core
        mask_bias = mask_ref[:, half * 256 : half * 256 + 256]
        for block in range(4):
            taken = [
                rest_ref[block * 2 : block * 2 + 2, source, :, part * 16 : part * 16 + 16, :].reshape(256, 128)
                for part in range(2)
            ]
            placed = nn(order, jnp.concatenate(taken, axis=1)) * log2e + mask_bias
            for head in range(4):
                for ah in range(2):
                    at = head * 64 + ah * 32
                    bias_ref[head, ah * 128 + block * 32 : ah * 128 + block * 32 + 32, half * 256 : half * 256 + 256] = (
                        placed[at : at + 32]
                    )
    heads = head_lanes(256)
    ones = jnp.ones((512, 128), bf16)

    def one_row(row, carry):
        own, other = own_ref[row], other_ref[row]
        projected = nn(own, w_in_ref[...])
        projected_other = nn(other, w_in_ref[:, 128:384])
        query = (projected[:, :128] * (32 ** (-0.5) * log2e)).astype(bf16)
        keys = jnp.concatenate([projected[:, 128:256].astype(bf16), projected_other[:, :128].astype(bf16)], axis=0)
        values = jnp.concatenate([projected[:, 256:384].astype(bf16), projected_other[:, 128:].astype(bf16)], axis=0)
        values = jnp.concatenate([values, ones], axis=1)
        gate = jax.nn.sigmoid(projected[:, 384:])
        attended = jnp.zeros((256, 128), f32)
        for head in range(4):
            scores = nt(jnp.where(heads[head], query, jnp.zeros_like(query)), keys) + bias_ref[head]
            weights = jnp.exp2(scores - jnp.max(scores, axis=1, keepdims=True)).astype(bf16)
            summed = nn(weights, values)
            attended = jnp.where(heads[head], summed[:, :128] / summed[:, 128:], attended)
        update = nn((attended * gate).astype(bf16), w_out_ref[...])
        result = (pair_ref[row].astype(f32) + update).astype(bf16)
        out_ref[row] = result
        normed = layer_norm(result.astype(f32)).astype(bf16)
        after_ref[row] = nt(next_ref[...], normed)
        return carry

    lax.fori_loop(0, 8, one_row, 0)
    largest, top = after_ref[0], jnp.full((8, 256), lowest, f32)
    for row in range(8):
        largest = jnp.maximum(largest, after_ref[row])
        top = jnp.maximum(top, jnp.where(kept_ref[row] > 0, after_ref[row], lowest))
    top = jnp.where(top > -1e38, top, largest).astype(bf16).astype(f32)
    for ah in range(2):
        extra_ref[ah, 32:40, :] = top[:, ah * 128 : ah * 128 + 128]
        for row in range(8):
            remains = after_ref[row] - top
            extra_ref[ah, row * 4 : row * 4 + 4, :] = remains[0:4, ah * 128 : ah * 128 + 128]


def end_kernel(core_ref, own_ref, other_ref, rest_ref, top_ref, mask_ref, w_in_ref, w_turned_ref, w_out_ref, pair_ref,
               out_ref, bias_ref):
    core = core_ref[0]
    to = lax.broadcasted_iota(jnp.int32, (256, 256), 0)
    key = to // 16 % 2 * 4 + to // 32 % 2 * 2 + to // 8 % 2
    place = to % 8 * 32 + key * 4 + to // 64
    order = (lax.broadcasted_iota(jnp.int32, (256, 256), 1) == place).astype(f32).astype(bf16)
    to = lax.broadcasted_iota(jnp.int32, (256, 64), 0)
    order_top = (lax.broadcasted_iota(jnp.int32, (256, 64), 1) == to % 8 * 8 + to // 64).astype(f32).astype(bf16)
    for block in range(8):
        rest = jnp.concatenate([rest_ref[block, t].reshape(256, 128) for t in range(2)], axis=1)
        top = jnp.concatenate([top_ref[block, t].reshape(64, 128).astype(bf16) for t in range(2)], axis=1)
        placed = (nn(order, rest) + nn(order_top, top)) * log2e
        for ah in range(2):
            half = core if ah == 0 else 1 - core
            for n5 in range(2):
                rows = pl.ds(pl.multiple_of(half * 256 + n5 * 128 + block * 16, 16), 16)
                mask_bias = mask_ref[rows, :]
                for head in range(4):
                    at = head * 64 + ah * 32 + n5 * 16
                    bias_ref[head, rows, :] = placed[at : at + 16] + mask_bias
    heads = head_lanes(512)
    ones = jnp.ones((16, 512), bf16)

    def one_column(column, carry):
        own, other = own_ref[column], other_ref[column]
        both = jnp.concatenate([own, other], axis=0)
        query = (nn(own, w_in_ref[:, :128]) * (32 ** (-0.5) * log2e)).astype(bf16)
        keys = nn(both, w_in_ref[:, 128:256]).astype(bf16)
        values = nt(w_turned_ref[:128], both).astype(bf16)
        gate = jax.nn.sigmoid(nt(w_turned_ref[128:], own))
        attended = []
        for head in range(4):
            scores = nt(jnp.where(heads[head], keys, jnp.zeros_like(keys)), query) + bias_ref[head]
            weights = jnp.exp2(scores - jnp.max(scores, axis=0, keepdims=True)).astype(bf16)
            summed = nn(jnp.concatenate([values[head * 32 : head * 32 + 32], ones], axis=0), weights)
            attended.append(summed[:32] / summed[32:33])
        attended = (jnp.concatenate(attended, axis=0) * gate).astype(bf16)
        update = dot(attended, w_out_ref[...], ((0,), (0,)))
        out_ref[column] = (pair_ref[column].astype(f32) + update).astype(bf16)
        return carry

    lax.fori_loop(0, 8, one_column, 0)


def call(kernel, in_kinds, outs, scratch, flops):
    spaces = {"s": pltpu.SMEM, "v": pltpu.VMEM}
    return pl.pallas_call(
        kernel,
        out_shape=outs,
        in_specs=[pl.BlockSpec(memory_space=spaces[kind]) for kind in in_kinds],
        out_specs=jax.tree.map(lambda _: pl.BlockSpec(memory_space=pltpu.VMEM), outs),
        scratch_shapes=scratch,
        compiler_params=pltpu.CompilerParams(vmem_limit_bytes=40 * 2**20),
        cost_estimate=pl.CostEstimate(flops=flops, bytes_accessed=4 * 2**20, transcendentals=4 * 2**20),
    )


def body(pair, mask, tri_in, tri_out, start_in, start_bias, start_out, end_in, end_bias, end_out):
    q = lax.axis_index(("xl", "y"))
    core = lax.axis_index("core")
    c = lax.axis_index(("z", "xh"))
    maskf = mask.astype(f32)

    pieces = pair.reshape(4, 8, 2, 32, 128).transpose(2, 1, 0, 3, 4).reshape(16, 128, 128)
    pair_rows = swap(pieces, same_q).reshape(2, 8, 4, 2, 16, 128).transpose(0, 2, 3, 1, 4, 5).reshape(2048, 128)

    normed = layer_norm(pair.astype(f32)).astype(bf16).reshape(2048, 128)
    terms = dot(tri_in[:, :512], normed, ((0,), (1,)))
    row_mask = lax.dynamic_slice_in_dim(maskf, (2 * q + core) * 32, 32)
    col_mask = lax.dynamic_slice_in_dim(maskf, c * 64, 64)
    pair_mask = (row_mask[:, None] * col_mask[None, :]).reshape(1, 2048)
    left = (jax.nn.sigmoid(terms[:128]) * terms[128:256] * pair_mask).astype(bf16)
    right = (jax.nn.sigmoid(terms[256:384]) * terms[384:512] * pair_mask).astype(bf16)
    both = jnp.concatenate([left.reshape(128, 16, 128), right.reshape(128, 16, 128)], axis=1)
    both = swap(both, everyone).reshape(16, 8, 2, 32, 64).transpose(2, 0, 3, 1, 4).reshape(2, 512, 512)
    combined = dot(both[0], both[1], ((1,), (1,))).astype(bf16)
    pieces = combined.reshape(8, 2, 4, 8, 8, 2, 2, 16).transpose(0, 5, 3, 1, 2, 6, 4, 7).reshape(128, 16, 128)
    combined = swap(pieces, everyone).reshape(128, 2048).astype(f32)

    mixed = layer_norm(combined, 0).astype(bf16)
    update = dot(mixed, tri_out, ((0,), (0,)))
    normed_rows = layer_norm(pair_rows.astype(f32)).astype(bf16)
    gate = jax.nn.sigmoid(dot(normed_rows, tri_in[:, 512:], ((1,), (0,))))
    pair_one = (pair_rows.astype(f32) + gate * update).astype(bf16)

    normed = layer_norm(pair_one.astype(f32)).astype(bf16)
    other = lax.ppermute(normed, "core", [(0, 1), (1, 0)])
    halves = mask.reshape(8, 2, 2, 16).transpose(1, 2, 0, 3).reshape(2, 256)
    halves = jnp.concatenate([lax.dynamic_slice_in_dim(halves, place, 1) for place in (core, 1 - core)], axis=1)
    kept = halves.reshape(2, 1, 1, 256) > 0
    bias = dot(start_bias, jnp.stack([normed, other]), ((0,), (2,))).reshape(4, 2, 8, 256).transpose(1, 0, 2, 3)
    top = jnp.max(jnp.where(kept, bias, lowest), axis=(0, 3), keepdims=True)
    top = jnp.where(top > -1e38, top, jnp.max(bias, axis=(0, 3), keepdims=True))
    rest = (bias - top)[0].astype(bf16)
    rest = rest.reshape(4, 2, 4, 2, 128).transpose(1, 3, 2, 0, 4).reshape(1, 2, 1, 32, 128)
    pieces = jnp.broadcast_to(rest, (8, 2, 8, 32, 128)).reshape(128, 32, 128)
    rest = swap(pieces, everyone).reshape(8, 2, 8, 32, 128)
    own_rows = lax.dynamic_index_in_dim(mask.reshape(8, 2, 4, 8), c, 3, False)
    own_rows = lax.dynamic_index_in_dim(own_rows, q, 0, False).reshape(8)
    here = core.astype(jnp.int32).reshape(1)
    next_bias = jnp.pad(end_bias.T, ((0, 4), (0, 0)))
    pair_two, extra = call(
        start_kernel,
        "ssvvvvvvvv",
        (jax.ShapeDtypeStruct((8, 256, 128), bf16), jax.ShapeDtypeStruct((2, 40, 128), f32)),
        [pltpu.VMEM((4, 256, 512), f32), pltpu.VMEM((8, 8, 256), f32)],
        3 * 10**9,
    )(
        here,
        own_rows,
        normed.reshape(8, 256, 128),
        other.reshape(8, 256, 128),
        rest,
        (halves.astype(f32) - 1.0) * (1000000000.0 * log2e),
        start_in,
        start_out,
        pair_one.reshape(8, 256, 128),
        next_bias,
    )

    extra = jnp.broadcast_to(extra.astype(bf16)[None, :, None], (8, 2, 8, 40, 128)).reshape(128, 40, 128)
    pieces = pair_two.reshape(2, 2, 2, 2, 8, 2, 8, 128).transpose(6, 1, 4, 3, 5, 0, 2, 7).reshape(128, 16, 128)
    pieces = swap(jnp.concatenate([pieces, extra], axis=1), everyone)
    pair_two = pieces[:, :16].reshape(8, 2, 8, 4, 2, 2, 128).transpose(1, 3, 4, 0, 5, 2, 6).reshape(2048, 128)
    rest = pieces[:, 16:48].reshape(8, 2, 8, 32, 128)
    top = pieces[:, 48:].astype(f32).reshape(8, 2, 8, 8, 128)

    normed = layer_norm(pair_two.astype(f32)).astype(bf16)
    other = lax.ppermute(normed, "core", [(0, 1), (1, 0)])
    halves = mask.reshape(8, 2, 2, 16).transpose(2, 1, 0, 3).reshape(2, 256)
    halves = jnp.concatenate([lax.dynamic_slice_in_dim(halves, place, 1) for place in (core, 1 - core)], axis=1)
    result = call(
        end_kernel,
        "svvvvvvvvv",
        jax.ShapeDtypeStruct((8, 256, 128), bf16),
        [pltpu.VMEM((4, 512, 256), f32)],
        3 * 10**9,
    )(
        here,
        normed.reshape(8, 256, 128),
        other.reshape(8, 256, 128),
        rest,
        top,
        ((halves.astype(f32) - 1.0) * (1000000000.0 * log2e)).reshape(512, 1),
        end_in,
        end_in[:, 256:].T,
        end_out,
        pair_two.reshape(8, 256, 128),
    )

    pieces = result.reshape(8, 2, 8, 16, 128).transpose(2, 1, 3, 0, 4).reshape(16, 128, 128)
    pieces = swap(pieces, same_c).reshape(8, 2, 16, 8, 128).transpose(1, 2, 3, 0, 4)
    return pieces.reshape(32, 64, 128)


def solution(mesh):
    parts = Mesh(mesh.devices.reshape(2, 4, 2, 4, 2), everyone)
    placed = P(("xl", "y", "core"), ("z", "xh"), None)
    in_specs = (placed,) + (P(),) * 9
    return jax.shard_map(body, mesh=parts, in_specs=in_specs, out_specs=placed, check_vma=False)
```

```python
import jax
import jax.numpy as jnp
from jax import lax
from jax.experimental import pallas as pl
from jax.experimental.pallas import tpu as pltpu
from jax.sharding import Mesh, PartitionSpec as P

everyone = ("xl", "y", "core", "z", "xh")
same_q = ("core", "z", "xh")
same_c = ("xl", "y", "core")
epsilon = 1e-05
bf16, f32 = jnp.bfloat16, jnp.float32
log2e = 1.4426950408889634
lowest = -3e38


def swap(pieces, axes):
    return lax.all_to_all(pieces, axes, 0, 0, tiled=True)


def layer_norm(values_in, axis=-1):
    average = jnp.mean(values_in, axis=axis, keepdims=True)
    centred = values_in - average
    variance = jnp.mean(centred * centred, axis=axis, keepdims=True)
    return centred * lax.rsqrt(variance + epsilon)


def dot(a, b, dims):
    return lax.dot_general(a, b, (dims, ((), ())), preferred_element_type=f32)


def nn(a, b):
    return dot(a, b, ((1,), (0,)))


def nt(a, b):
    return dot(a, b, ((1,), (1,)))


def head_lanes(rows):
    lanes = lax.broadcasted_iota(jnp.int32, (rows, 128), 1)
    return [(lanes >= 32 * head) & (lanes < 32 * head + 32) for head in range(4)]


def triangle_kernel(both_ref, out_ref, left_ref, right_ref):
    at = lax.broadcasted_iota(jnp.int32, (256, 256), 0)
    to = lax.broadcasted_iota(jnp.int32, (256, 256), 1)
    lanes = (at == to // 64 % 2 * 128 + to // 128 * 64 + to % 64).astype(f32).astype(bf16)
    for side, kept_ref in ((0, left_ref), (1, right_ref)):
        for pair_at in range(4):
            taken = [
                both_ref[:, :, pair_at * 2 + odd, side * 16 : side * 16 + 16, :].reshape(256, 128) for odd in range(2)
            ]
            moved = nn(jnp.concatenate(taken, axis=1), lanes).astype(bf16)
            for pi in range(2):
                kept_ref[pi, :, pair_at * 128 : pair_at * 128 + 128] = moved[:, pi * 128 : pi * 128 + 128]
    right = jnp.concatenate(
        [right_ref[pi].reshape(8, 2, 16, 512)[:, half].reshape(128, 512) for half in range(2) for pi in range(2)], axis=0
    )
    place = to * 0 + at // 2 % 2 * 128 + at // 64 * 32 + at // 4 % 2 * 16 + at % 2 * 8 + at // 8 % 8
    order = (to == place).astype(f32).astype(bf16)
    for block in range(2):
        taken = jnp.concatenate([left_ref[pi, block * 128 : block * 128 + 128, :] for pi in range(2)], axis=0)
        left = nn(order, taken).astype(bf16)
        combined = nt(left, right)
        for q in range(4):
            for half in range(2):
                piece = combined[q * 64 : q * 64 + 64, half * 256 : half * 256 + 256].reshape(8, 8, 256)
                piece = jnp.concatenate([piece[:, :, :128], piece[:, :, 128:]], axis=1)
                out_ref[block * 4 + q, half] = piece.astype(bf16)


def start_kernel(core_ref, kept_ref, own_ref, other_ref, rest_ref, mask_ref, w_in_ref, w_out_ref, pair_ref, next_ref,
                 out_ref, extra_ref, bias_ref, after_ref):
    core = core_ref[0]
    to = lax.broadcasted_iota(jnp.int32, (256, 256), 0)
    place = (to // 16 % 2 * 8 + to % 8) * 16 + (to // 32 % 2 * 2 + to // 8 % 2) * 4 + to // 64
    order = (lax.broadcasted_iota(jnp.int32, (256, 256), 1) == place).astype(f32).astype(bf16)
    for half in range(2):
        source = core if half == 0 else 1 - core
        mask_bias = mask_ref[:, half * 256 : half * 256 + 256]
        for block in range(4):
            taken = [
                rest_ref[block * 2 : block * 2 + 2, source, :, part * 16 : part * 16 + 16, :].reshape(256, 128)
                for part in range(2)
            ]
            placed = nn(order, jnp.concatenate(taken, axis=1)) * log2e + mask_bias
            for head in range(4):
                for ah in range(2):
                    at = head * 64 + ah * 32
                    bias_ref[head, ah * 128 + block * 32 : ah * 128 + block * 32 + 32, half * 256 : half * 256 + 256] = (
                        placed[at : at + 32]
                    )
    heads = head_lanes(256)
    ones = jnp.ones((512, 128), bf16)

    def one_row(row, carry):
        own, other = own_ref[:, row].reshape(256, 128), other_ref[:, row].reshape(256, 128)
        projected = nn(own, w_in_ref[...])
        projected_other = nn(other, w_in_ref[:, 128:384])
        query = (projected[:, :128] * (32 ** (-0.5) * log2e)).astype(bf16)
        keys = jnp.concatenate([projected[:, 128:256].astype(bf16), projected_other[:, :128].astype(bf16)], axis=0)
        values = jnp.concatenate([projected[:, 256:384].astype(bf16), projected_other[:, 128:].astype(bf16)], axis=0)
        values = jnp.concatenate([values, ones], axis=1)
        gate = jax.nn.sigmoid(projected[:, 384:])
        attended = jnp.zeros((256, 128), f32)
        for head in range(4):
            scores = nt(jnp.where(heads[head], query, jnp.zeros_like(query)), keys) + bias_ref[head]
            weights = jnp.exp2(scores - jnp.max(scores, axis=1, keepdims=True)).astype(bf16)
            summed = nn(weights, values)
            attended = jnp.where(heads[head], summed[:, :128] / summed[:, 128:], attended)
        update = nn((attended * gate).astype(bf16), w_out_ref[...])
        result = (pair_ref[:, row].reshape(256, 128).astype(f32) + update).astype(bf16)
        out_ref[:, row] = result.reshape(2, 128, 128)
        normed = layer_norm(result.astype(f32)).astype(bf16)
        after_ref[row] = nt(next_ref[...], normed)
        return carry

    lax.fori_loop(0, 8, one_row, 0)
    largest, top = after_ref[0], jnp.full((8, 256), lowest, f32)
    for row in range(8):
        largest = jnp.maximum(largest, after_ref[row])
        top = jnp.maximum(top, jnp.where(kept_ref[row] > 0, after_ref[row], lowest))
    top = jnp.where(top > -1e38, top, largest).astype(bf16).astype(f32)
    for ah in range(2):
        extra_ref[ah, 32:40, :] = top[:, ah * 128 : ah * 128 + 128]
        for row in range(8):
            remains = after_ref[row] - top
            extra_ref[ah, row * 4 : row * 4 + 4, :] = remains[0:4, ah * 128 : ah * 128 + 128]


def end_kernel(core_ref, own_ref, other_ref, rest_ref, top_ref, mask_ref, w_in_ref, w_turned_ref, w_out_ref, pair_ref,
               out_ref, bias_ref):
    core = core_ref[0]
    to = lax.broadcasted_iota(jnp.int32, (256, 256), 0)
    key = to // 16 % 2 * 4 + to // 32 % 2 * 2 + to // 8 % 2
    place = to % 8 * 32 + key * 4 + to // 64
    order = (lax.broadcasted_iota(jnp.int32, (256, 256), 1) == place).astype(f32).astype(bf16)
    to = lax.broadcasted_iota(jnp.int32, (256, 64), 0)
    order_top = (lax.broadcasted_iota(jnp.int32, (256, 64), 1) == to % 8 * 8 + to // 64).astype(f32).astype(bf16)
    for block in range(8):
        rest = jnp.concatenate([rest_ref[block, t].reshape(256, 128) for t in range(2)], axis=1)
        top = jnp.concatenate([top_ref[block, t].reshape(64, 128).astype(bf16) for t in range(2)], axis=1)
        placed = (nn(order, rest) + nn(order_top, top)) * log2e
        for ah in range(2):
            half = core if ah == 0 else 1 - core
            for n5 in range(2):
                rows = pl.ds(pl.multiple_of(half * 256 + n5 * 128 + block * 16, 16), 16)
                mask_bias = mask_ref[rows, :]
                for head in range(4):
                    at = head * 64 + ah * 32 + n5 * 16
                    bias_ref[head, rows, :] = placed[at : at + 16] + mask_bias
    heads = head_lanes(512)
    ones = jnp.ones((16, 512), bf16)

    def one_column(column, carry):
        own, other = own_ref[column], other_ref[column]
        both = jnp.concatenate([own, other], axis=0)
        query = (nn(own, w_in_ref[:, :128]) * (32 ** (-0.5) * log2e)).astype(bf16)
        keys = nn(both, w_in_ref[:, 128:256]).astype(bf16)
        values = nt(w_turned_ref[:128], both).astype(bf16)
        gate = jax.nn.sigmoid(nt(w_turned_ref[128:], own))
        attended = []
        for head in range(4):
            scores = nt(jnp.where(heads[head], keys, jnp.zeros_like(keys)), query) + bias_ref[head]
            weights = jnp.exp2(scores - jnp.max(scores, axis=0, keepdims=True)).astype(bf16)
            summed = nn(jnp.concatenate([values[head * 32 : head * 32 + 32], ones], axis=0), weights)
            attended.append(summed[:32] / summed[32:33])
        attended = (jnp.concatenate(attended, axis=0) * gate).astype(bf16)
        update = dot(attended, w_out_ref[...], ((0,), (0,)))
        out_ref[column] = (pair_ref[column].astype(f32) + update).astype(bf16)
        return carry

    lax.fori_loop(0, 8, one_column, 0)


def call(kernel, in_kinds, outs, scratch, flops):
    spaces = {"s": pltpu.SMEM, "v": pltpu.VMEM}
    return pl.pallas_call(
        kernel,
        out_shape=outs,
        in_specs=[pl.BlockSpec(memory_space=spaces[kind]) for kind in in_kinds],
        out_specs=jax.tree.map(lambda _: pl.BlockSpec(memory_space=pltpu.VMEM), outs),
        scratch_shapes=scratch,
        compiler_params=pltpu.CompilerParams(vmem_limit_bytes=40 * 2**20),
        cost_estimate=pl.CostEstimate(flops=flops, bytes_accessed=4 * 2**20, transcendentals=4 * 2**20),
    )


def body(pair, mask, tri_in, tri_out, start_in, start_bias, start_out, end_in, end_bias, end_out):
    q = lax.axis_index(("xl", "y"))
    core = lax.axis_index("core")
    c = lax.axis_index(("z", "xh"))
    maskf = mask.astype(f32)

    pieces = pair.reshape(4, 8, 2, 32, 128).transpose(2, 1, 0, 3, 4).reshape(16, 128, 128)
    pair_rows = swap(pieces, same_q).reshape(2, 8, 4, 2, 16, 128).transpose(3, 0, 2, 1, 4, 5).reshape(2048, 128)

    normed = layer_norm(pair.astype(f32)).astype(bf16)
    normed = normed.reshape(2, 16, 64, 128).transpose(1, 0, 2, 3).reshape(2048, 128)
    terms = dot(tri_in[:, :512], normed, ((0,), (1,)))
    row_mask = lax.dynamic_slice_in_dim(maskf, (2 * q + core) * 32, 32)
    col_mask = lax.dynamic_slice_in_dim(maskf, c * 64, 64)
    pair_mask = (row_mask.reshape(2, 16).T[:, :, None] * col_mask).reshape(1, 2048)
    left = (jax.nn.sigmoid(terms[:128]) * terms[128:256] * pair_mask).astype(bf16)
    right = (jax.nn.sigmoid(terms[256:384]) * terms[384:512] * pair_mask).astype(bf16)
    both = jnp.concatenate([left.reshape(128, 16, 128), right.reshape(128, 16, 128)], axis=1)
    both = swap(both, everyone).reshape(8, 2, 8, 32, 128)
    pieces = call(
        triangle_kernel,
        "v",
        jax.ShapeDtypeStruct((8, 2, 8, 16, 128), bf16),
        [pltpu.VMEM((2, 256, 512), bf16)] * 2,
        3 * 10**8,
    )(both)
    combined = swap(pieces.reshape(128, 16, 128), everyone).reshape(128, 2048).astype(f32)

    mixed = layer_norm(combined, 0).astype(bf16)
    update = dot(mixed, tri_out, ((0,), (0,)))
    normed_rows = layer_norm(pair_rows.astype(f32)).astype(bf16)
    gate = jax.nn.sigmoid(dot(normed_rows, tri_in[:, 512:], ((1,), (0,))))
    pair_one = (pair_rows.astype(f32) + gate * update).astype(bf16)

    normed = layer_norm(pair_one.astype(f32)).astype(bf16)
    other = lax.ppermute(normed, "core", [(0, 1), (1, 0)])
    halves = mask.reshape(8, 2, 2, 16).transpose(1, 2, 0, 3).reshape(2, 256)
    halves = jnp.concatenate([lax.dynamic_slice_in_dim(halves, place, 1) for place in (core, 1 - core)], axis=1)
    kept = halves.reshape(2, 1, 1, 2, 128) > 0
    bias = dot(start_bias, jnp.stack([normed, other]), ((0,), (2,))).reshape(4, 2, 2, 8, 128).transpose(1, 0, 3, 2, 4)
    top = jnp.max(jnp.where(kept, bias, lowest), axis=(0, 3, 4), keepdims=True)
    top = jnp.where(top > -1e38, top, jnp.max(bias, axis=(0, 3, 4), keepdims=True))
    rest = (bias - top)[0].astype(bf16)
    rest = rest.reshape(4, 2, 4, 2, 128).transpose(1, 3, 2, 0, 4).reshape(1, 2, 1, 32, 128)
    pieces = jnp.broadcast_to(rest, (8, 2, 8, 32, 128)).reshape(128, 32, 128)
    rest = swap(pieces, everyone).reshape(8, 2, 8, 32, 128)
    own_rows = lax.dynamic_index_in_dim(mask.reshape(8, 2, 4, 8), c, 3, False)
    own_rows = lax.dynamic_index_in_dim(own_rows, q, 0, False).reshape(8)
    here = core.astype(jnp.int32).reshape(1)
    next_bias = jnp.pad(end_bias.T, ((0, 4), (0, 0)))
    pair_two, extra = call(
        start_kernel,
        "ssvvvvvvvv",
        (jax.ShapeDtypeStruct((2, 8, 128, 128), bf16), jax.ShapeDtypeStruct((2, 40, 128), f32)),
        [pltpu.VMEM((4, 256, 512), f32), pltpu.VMEM((8, 8, 256), f32)],
        3 * 10**9,
    )(
        here,
        own_rows,
        normed.reshape(2, 8, 128, 128),
        other.reshape(2, 8, 128, 128),
        rest,
        (halves.astype(f32) - 1.0) * (1000000000.0 * log2e),
        start_in,
        start_out,
        pair_one.reshape(2, 8, 128, 128),
        next_bias,
    )

    extra = jnp.broadcast_to(extra.astype(bf16)[None, :, None], (8, 2, 8, 40, 128)).reshape(128, 40, 128)
    pieces = pair_two.reshape(2, 2, 2, 2, 8, 2, 8, 128).transpose(6, 2, 4, 0, 5, 1, 3, 7).reshape(128, 16, 128)
    pieces = swap(jnp.concatenate([pieces, extra], axis=1), everyone)
    pair_two = pieces[:, :16].reshape(8, 2, 8, 4, 2, 2, 128).transpose(1, 3, 4, 0, 5, 2, 6).reshape(2048, 128)
    rest = pieces[:, 16:48].reshape(8, 2, 8, 32, 128)
    top = pieces[:, 48:].astype(f32).reshape(8, 2, 8, 8, 128)

    normed = layer_norm(pair_two.astype(f32)).astype(bf16)
    other = lax.ppermute(normed, "core", [(0, 1), (1, 0)])
    halves = mask.reshape(8, 2, 2, 16).transpose(2, 1, 0, 3).reshape(2, 256)
    halves = jnp.concatenate([lax.dynamic_slice_in_dim(halves, place, 1) for place in (core, 1 - core)], axis=1)
    result = call(
        end_kernel,
        "svvvvvvvvv",
        jax.ShapeDtypeStruct((8, 256, 128), bf16),
        [pltpu.VMEM((4, 512, 256), f32)],
        3 * 10**9,
    )(
        here,
        normed.reshape(8, 256, 128),
        other.reshape(8, 256, 128),
        rest,
        top,
        ((halves.astype(f32) - 1.0) * (1000000000.0 * log2e)).reshape(512, 1),
        end_in,
        end_in[:, 256:].T,
        end_out,
        pair_two.reshape(8, 256, 128),
    )

    pieces = result.reshape(8, 2, 8, 16, 128).transpose(2, 1, 3, 0, 4).reshape(16, 128, 128)
    pieces = swap(pieces, same_c).reshape(8, 2, 16, 8, 128).transpose(1, 2, 3, 0, 4)
    return pieces.reshape(32, 64, 128)


def solution(mesh):
    parts = Mesh(mesh.devices.reshape(2, 4, 2, 4, 2), everyone)
    placed = P(("xl", "y", "core"), ("z", "xh"), None)
    in_specs = (placed,) + (P(),) * 9
    return jax.shard_map(body, mesh=parts, in_specs=in_specs, out_specs=placed, check_vma=False)
```

```python
import jax
import jax.numpy as jnp
from jax import lax
from jax.experimental import pallas as pl
from jax.experimental.pallas import tpu as pltpu
from jax.sharding import Mesh, PartitionSpec as P

everyone = ("xl", "y", "core", "z", "xh")
by_row = ("z", "xh", "core")
same_c = ("xl", "y", "core")
epsilon = 1e-05
bf16, f32 = jnp.bfloat16, jnp.float32
log2e = 1.4426950408889634
lowest = -3e38


def swap(pieces, axes):
    return lax.all_to_all(pieces, axes, 0, 0, tiled=True)


def layer_norm(values_in, axis=-1):
    average = jnp.mean(values_in, axis=axis, keepdims=True)
    centred = values_in - average
    variance = jnp.mean(centred * centred, axis=axis, keepdims=True)
    return centred * lax.rsqrt(variance + epsilon)


def dot(a, b, dims):
    return lax.dot_general(a, b, (dims, ((), ())), preferred_element_type=f32)


def nn(a, b):
    return dot(a, b, ((1,), (0,)))


def nt(a, b):
    return dot(a, b, ((1,), (1,)))


def head_lanes(rows):
    lanes = lax.broadcasted_iota(jnp.int32, (rows, 128), 1)
    return [(lanes >= 32 * head) & (lanes < 32 * head + 32) for head in range(4)]


def terms_kernel(pair_ref, w_in_ref, mask_ref, left_ref, right_ref, held_ref):
    for step in range(8):
        rows = [(place % 8) * 4 + ah * 2 + place // 8 for place in (2 * step, 2 * step + 1) for ah in range(2)]
        tokens = jnp.concatenate([pair_ref[row] for row in rows], axis=0).astype(f32)
        terms = dot(w_in_ref[...], layer_norm(tokens).astype(bf16), ((0,), (1,)))
        for side in range(2):
            at = side * 256
            kept = jax.nn.sigmoid(terms[at : at + 128]) * terms[at + 128 : at + 256] * mask_ref[step : step + 1, :]
            for odd in range(2):
                held_ref[side, pl.ds(2 * step + odd, 128, stride=16), :] = kept[:, odd * 128 : odd * 128 + 128]
    left_ref[...] = held_ref[0].astype(bf16).reshape(128, 16, 128)
    right_ref[...] = held_ref[1].astype(bf16).reshape(128, 16, 128)


def triangle_kernel(both_ref, out_ref, left_ref, right_ref):
    at = lax.broadcasted_iota(jnp.int32, (256, 256), 0)
    to = lax.broadcasted_iota(jnp.int32, (256, 256), 1)
    lanes = (at == to // 64 % 2 * 128 + to // 128 * 64 + to % 64).astype(f32).astype(bf16)
    for side, kept_ref in ((0, left_ref), (1, right_ref)):
        for pair_at in range(4):
            taken = [
                both_ref[:, :, pair_at * 2 + odd, side * 16 : side * 16 + 16, :].reshape(256, 128) for odd in range(2)
            ]
            moved = nn(jnp.concatenate(taken, axis=1), lanes).astype(bf16)
            for pi in range(2):
                kept_ref[pi, :, pair_at * 128 : pair_at * 128 + 128] = moved[:, pi * 128 : pi * 128 + 128]
    place = to * 0 + at // 8 % 8 * 32 + at // 128 * 16 + at // 64 % 2 * 8 + at % 8
    order = (to == place).astype(f32).astype(bf16)
    right = [nn(order, right_ref[pi]).astype(bf16) for pi in range(2)]
    right = jnp.concatenate([right[pi][half * 128 : half * 128 + 128] for half in range(2) for pi in range(2)], axis=0)
    place = to * 0 + at // 2 % 2 * 128 + at // 64 * 32 + at // 4 % 2 * 16 + at % 2 * 8 + at // 8 % 8
    order = (to == place).astype(f32).astype(bf16)
    for block in range(2):
        taken = jnp.concatenate([left_ref[pi, block * 128 : block * 128 + 128, :] for pi in range(2)], axis=0)
        left = nn(order, taken).astype(bf16)
        combined = nt(left, right)
        for q in range(4):
            for half in range(2):
                piece = combined[q * 64 : q * 64 + 64, half * 256 : half * 256 + 256].reshape(8, 8, 256)
                piece = jnp.concatenate([piece[:, :, :128], piece[:, :, 128:]], axis=1)
                out_ref[block * 4 + q, half] = piece.astype(bf16)


def mix_kernel(combined_ref, pair_ref, gate_ref, w_ref, one_ref, normed_ref, held_ref):
    held_ref[...] = layer_norm(combined_ref[...].astype(f32), 0).reshape(2048, 128)
    for step in range(8):
        mixed = [held_ref[pl.ds(2 * step + odd, 128, stride=16), :] for odd in range(2)]
        update = dot(jnp.concatenate(mixed, axis=1).astype(bf16), w_ref[...], ((0,), (0,)))
        rows = slice(2 * step, 2 * step + 2)
        pair = pair_ref[rows].reshape(256, 128).astype(f32)
        one = (pair + gate_ref[rows].reshape(256, 128) * update).astype(bf16)
        one_ref[rows] = one.reshape(2, 128, 128)
        normed_ref[rows] = layer_norm(one.astype(f32)).astype(bf16).reshape(2, 128, 128)


def bias_kernel(own_ref, other_ref, w_ref, mask_ref, out_ref, held_ref):
    sides = [nt(w_ref[...], side[...].reshape(2048, 128)) for side in (own_ref, other_ref)]
    for row in range(8):
        parts = [side[:, ah * 1024 + row * 128 : ah * 1024 + row * 128 + 128] for side in sides for ah in range(2)]
        largest, top = parts[0], jnp.full((8, 128), lowest, f32)
        for place, part in enumerate(parts):
            largest = jnp.maximum(largest, part)
            top = jnp.maximum(top, jnp.where(mask_ref[:, place * 128 : place * 128 + 128] > 0, part, lowest))
        top = jnp.max(top, axis=1, keepdims=True)
        top = jnp.where(top > -1e38, top, jnp.max(largest, axis=1, keepdims=True))
        for ah in range(2):
            at = ah * 16 + row % 4 * 4
            held_ref[row // 4, at : at + 4, :] = (parts[ah] - top)[0:4]
    out_ref[...] = jnp.broadcast_to(held_ref[...].astype(bf16)[None, :, None], (8, 2, 8, 32, 128))


def start_kernel(core_ref, kept_ref, own_ref, other_ref, rest_ref, mask_ref, w_in_ref, w_out_ref, pair_ref, next_ref,
                 out_ref, extra_ref, bias_ref, after_ref):
    core = core_ref[0]
    to = lax.broadcasted_iota(jnp.int32, (256, 256), 0)
    place = (to // 8 % 2 * 8 + to % 8) * 16 + (to // 16 % 4) * 4 + to // 64
    order = (lax.broadcasted_iota(jnp.int32, (256, 256), 1) == place).astype(f32).astype(bf16)
    for half in range(2):
        source = core if half == 0 else 1 - core
        mask_bias = mask_ref[:, half * 256 : half * 256 + 256]
        for block in range(4):
            taken = [
                rest_ref[block * 2 : block * 2 + 2, source, :, part * 16 : part * 16 + 16, :].reshape(256, 128)
                for part in range(2)
            ]
            placed = nn(order, jnp.concatenate(taken, axis=1)) * log2e + mask_bias
            for head in range(4):
                for part in range(4):
                    at = head * 64 + part * 16
                    bias_ref[head, part * 64 + block * 16 : part * 64 + block * 16 + 16, half * 256 : half * 256 + 256] = (
                        placed[at : at + 16]
                    )
    heads = head_lanes(256)
    ones = jnp.ones((512, 128), bf16)

    def one_row(row, carry):
        own, other = own_ref[:, row].reshape(256, 128), other_ref[:, row].reshape(256, 128)
        projected = nn(own, w_in_ref[...])
        projected_other = nn(other, w_in_ref[:, 128:384])
        query = (projected[:, :128] * (32 ** (-0.5) * log2e)).astype(bf16)
        keys = jnp.concatenate([projected[:, 128:256].astype(bf16), projected_other[:, :128].astype(bf16)], axis=0)
        values = jnp.concatenate([projected[:, 256:384].astype(bf16), projected_other[:, 128:].astype(bf16)], axis=0)
        values = jnp.concatenate([values, ones], axis=1)
        gate = jax.nn.sigmoid(projected[:, 384:])
        queries = jnp.concatenate([jnp.where(lanes, query, jnp.zeros_like(query)) for lanes in heads], axis=0)
        scores = nt(queries, keys)
        attended = jnp.zeros((256, 128), f32)
        for head in range(4):
            part = scores[head * 256 : head * 256 + 256] + bias_ref[head]
            weights = jnp.exp2(part - jnp.max(part, axis=1, keepdims=True)).astype(bf16)
            summed = nn(weights, values)
            attended = jnp.where(heads[head], summed[:, :128] / summed[:, 128:], attended)
        update = nn((attended * gate).astype(bf16), w_out_ref[...])
        result = (pair_ref[:, row].reshape(256, 128).astype(f32) + update).astype(bf16)
        out_ref[:, row] = result.reshape(2, 128, 128)
        return carry

    lax.fori_loop(0, 8, one_row, 0, unroll=2)
    for row in range(8):
        normed = layer_norm(out_ref[:, row].reshape(256, 128).astype(f32)).astype(bf16)
        after_ref[row] = nt(next_ref[...], normed)
    largest, top = after_ref[0], jnp.full((8, 256), lowest, f32)
    for row in range(8):
        largest = jnp.maximum(largest, after_ref[row])
        top = jnp.maximum(top, jnp.where(kept_ref[row] > 0, after_ref[row], lowest))
    top = jnp.where(top > -1e38, top, largest).astype(bf16).astype(f32)
    for ah in range(2):
        extra_ref[ah, 32:40, :] = top[:, ah * 128 : ah * 128 + 128]
        for row in range(8):
            remains = after_ref[row] - top
            extra_ref[ah, row * 4 : row * 4 + 4, :] = remains[0:4, ah * 128 : ah * 128 + 128]


def end_kernel(core_ref, pieces_ref, other_ref, top_ref, mask_ref, w_in_ref, w_turned_ref, w_out_ref, out_ref, bias_ref,
               own_ref, both_ref):
    core = core_ref[0]
    to = lax.broadcasted_iota(jnp.int32, (256, 256), 0)
    key = to // 16 % 2 * 4 + to // 32 % 2 * 2 + to // 8 % 2
    place = to % 8 * 32 + key * 4 + to // 64
    order = (lax.broadcasted_iota(jnp.int32, (256, 256), 1) == place).astype(f32).astype(bf16)
    to = lax.broadcasted_iota(jnp.int32, (256, 64), 0)
    order_top = (lax.broadcasted_iota(jnp.int32, (256, 64), 1) == to % 8 * 8 + to // 64).astype(f32).astype(bf16)
    for block in range(8):
        rest = jnp.concatenate([pieces_ref[block, t, :, 16:48, :].reshape(256, 128) for t in range(2)], axis=1)
        top = jnp.concatenate([top_ref[block, t].reshape(64, 128).astype(bf16) for t in range(2)], axis=1)
        placed = (nn(order, rest) + nn(order_top, top)) * log2e
        for ah in range(2):
            half = core if ah == 0 else 1 - core
            for part in range(4):
                rows = pl.ds(pl.multiple_of(half * 256 + part * 64 + block * 8, 8), 8)
                mask_bias = mask_ref[rows, :]
                for head in range(4):
                    at = head * 64 + ah * 32 + part * 8
                    bias_ref[head, rows, :] = placed[at : at + 8] + mask_bias
    for block in range(8):
        for t in range(2):
            rows = slice(block * 128, block * 128 + 128)
            own_ref[t, rows, :] = pieces_ref[block, t, :, 0:16, :].astype(f32).reshape(128, 128)
            both_ref[t, rows, :] = other_ref[block, t].astype(f32).reshape(128, 128)
    heads = head_lanes(512)
    ones = jnp.ones((16, 512), bf16)

    def taken(from_ref, column):
        return jnp.concatenate(
            [from_ref[column // 4, pl.ds(column % 4 * 4 + part, 64, stride=16), :] for part in range(4)], axis=0
        )

    def one_column(column, carry):
        pair = taken(own_ref, column)
        own = layer_norm(pair).astype(bf16)
        other = layer_norm(taken(both_ref, column)).astype(bf16)
        both = jnp.concatenate([own, other], axis=0)
        query = (nn(own, w_in_ref[:, :128]) * (32 ** (-0.5) * log2e)).astype(bf16)
        keys = nn(both, w_in_ref[:, 128:256]).astype(bf16)
        values = nt(w_turned_ref[:128], both).astype(bf16)
        gate = jax.nn.sigmoid(nt(w_turned_ref[128:], own))
        stacked = jnp.concatenate([jnp.where(lanes, keys, jnp.zeros_like(keys)) for lanes in heads], axis=0)
        scores = nt(stacked, query)
        attended = []
        for head in range(4):
            part = scores[head * 512 : head * 512 + 512] + bias_ref[head]
            weights = jnp.exp2(part - jnp.max(part, axis=0, keepdims=True)).astype(bf16)
            summed = nn(jnp.concatenate([values[head * 32 : head * 32 + 32], ones], axis=0), weights)
            attended.append(summed[:32] / summed[32:33])
        attended = (jnp.concatenate(attended, axis=0) * gate).astype(bf16)
        update = dot(attended, w_out_ref[...], ((0,), (0,)))
        out_ref[column] = (pair + update).astype(bf16)
        return carry

    lax.fori_loop(0, 8, one_column, 0, unroll=2)


def call(kernel, in_kinds, outs, scratch, flops):
    spaces = {"s": pltpu.SMEM, "v": pltpu.VMEM}
    return pl.pallas_call(
        kernel,
        out_shape=outs,
        in_specs=[pl.BlockSpec(memory_space=spaces[kind]) for kind in in_kinds],
        out_specs=jax.tree.map(lambda _: pl.BlockSpec(memory_space=pltpu.VMEM), outs),
        scratch_shapes=scratch,
        compiler_params=pltpu.CompilerParams(vmem_limit_bytes=40 * 2**20),
        cost_estimate=pl.CostEstimate(flops=flops, bytes_accessed=4 * 2**20, transcendentals=4 * 2**20),
    )


def body(pair, mask, tri_in, tri_out, start_in, start_bias, start_out, end_in, end_bias, end_out):
    q = lax.axis_index(("xl", "y"))
    core = lax.axis_index("core")
    c = lax.axis_index(("z", "xh"))
    maskf = mask.astype(f32)

    rows = swap(pair.reshape(16, 128, 128), by_row).reshape(8, 2, 2, 2, 32, 128)

    row_mask = lax.dynamic_slice_in_dim(maskf, (2 * q + core) * 32, 32)
    col_mask = lax.dynamic_slice_in_dim(maskf, c * 64, 64)
    pair_mask = (row_mask.reshape(8, 2, 2).transpose(2, 0, 1).reshape(16, 2, 1) * col_mask).reshape(8, 256)
    both = call(
        terms_kernel,
        "vvv",
        (jax.ShapeDtypeStruct((128, 16, 128), bf16),) * 2,
        [pltpu.VMEM((2, 2048, 128), f32)],
        3 * 10**8,
    )(pair, tri_in[:, :512], pair_mask)
    both = jnp.concatenate(both, axis=1)
    both, rows = lax.optimization_barrier((both, rows))
    both = swap(both, everyone).reshape(8, 2, 8, 32, 128)
    kept = lax.dynamic_index_in_dim(rows, core, 3, False)
    given = lax.ppermute(lax.dynamic_index_in_dim(rows, 1 - core, 3, False), "core", [(0, 1), (1, 0)])
    rows = jnp.stack([jnp.where(core == 0, kept, given), jnp.where(core == 0, given, kept)])
    rows = rows.reshape(2, 8, 2, 2, 8, 2, 2, 128).transpose(5, 2, 0, 3, 6, 1, 4, 7)
    pair_rows = rows.reshape(2048, 128)
    pieces = call(
        triangle_kernel,
        "v",
        jax.ShapeDtypeStruct((8, 2, 8, 16, 128), bf16),
        [pltpu.VMEM((2, 256, 512), bf16)] * 2,
        3 * 10**8,
    )(both)
    combined = swap(pieces.reshape(128, 16, 128), everyone)

    normed_rows = layer_norm(pair_rows.astype(f32)).astype(bf16)
    gate = jax.nn.sigmoid(dot(normed_rows, tri_in[:, 512:], ((1,), (0,))))
    pair_one, normed = call(
        mix_kernel,
        "vvvv",
        (jax.ShapeDtypeStruct((16, 128, 128), bf16),) * 2,
        [pltpu.VMEM((2048, 128), f32)],
        2 * 10**8,
    )(combined, pair_rows.reshape(16, 128, 128), gate.reshape(16, 128, 128), tri_out)

    other = lax.ppermute(normed, "core", [(0, 1), (1, 0)])
    halves = mask.reshape(8, 2, 8, 2, 2).transpose(1, 3, 4, 0, 2).reshape(2, 256)
    halves = jnp.concatenate([lax.dynamic_slice_in_dim(halves, place, 1) for place in (core, 1 - core)], axis=1)
    pieces = call(
        bias_kernel,
        "vvvv",
        jax.ShapeDtypeStruct((8, 2, 8, 32, 128), bf16),
        [pltpu.VMEM((2, 32, 128), f32)],
        10**8,
    )(
        normed.reshape(2, 8, 128, 128),
        other.reshape(2, 8, 128, 128),
        jnp.pad(start_bias.T, ((0, 4), (0, 0))),
        halves.astype(f32),
    )
    rest = swap(pieces.reshape(128, 32, 128), everyone).reshape(8, 2, 8, 32, 128)
    own_rows = lax.dynamic_index_in_dim(mask.reshape(8, 2, 8, 4), c, 2, False)
    own_rows = lax.dynamic_index_in_dim(own_rows, q, 0, False).reshape(8)
    here = core.astype(jnp.int32).reshape(1)
    next_bias = jnp.pad(end_bias.T, ((0, 4), (0, 0)))
    pair_two, extra = call(
        start_kernel,
        "ssvvvvvvvv",
        (jax.ShapeDtypeStruct((2, 8, 128, 128), bf16), jax.ShapeDtypeStruct((2, 40, 128), f32)),
        [pltpu.VMEM((4, 256, 512), f32), pltpu.VMEM((8, 8, 256), f32)],
        3 * 10**9,
    )(
        here,
        own_rows,
        normed.reshape(2, 8, 128, 128),
        other.reshape(2, 8, 128, 128),
        rest,
        (halves.astype(f32) - 1.0) * (1000000000.0 * log2e),
        start_in,
        start_out,
        pair_one.reshape(2, 8, 128, 128),
        next_bias,
    )

    extra = jnp.broadcast_to(extra.astype(bf16)[None, :, None], (8, 2, 8, 40, 128)).reshape(128, 40, 128)
    pieces = pair_two.reshape(2, 2, 2, 2, 2, 8, 8, 128).transpose(6, 2, 5, 0, 4, 1, 3, 7).reshape(128, 16, 128)
    pieces = swap(jnp.concatenate([pieces, extra], axis=1), everyone)
    other = lax.ppermute(pieces[:, :16], "core", [(0, 1), (1, 0)])
    top = pieces[:, 48:].astype(f32).reshape(8, 2, 8, 8, 128)

    halves = mask.reshape(8, 2, 8, 2, 2).transpose(3, 1, 4, 0, 2).reshape(2, 256)
    halves = jnp.concatenate([lax.dynamic_slice_in_dim(halves, place, 1) for place in (core, 1 - core)], axis=1)
    result = call(
        end_kernel,
        "svvvvvvv",
        jax.ShapeDtypeStruct((8, 256, 128), bf16),
        [pltpu.VMEM((4, 512, 256), f32)] + [pltpu.VMEM((2, 1024, 128), f32)] * 2,
        3 * 10**9,
    )(
        here,
        pieces.reshape(8, 2, 8, 56, 128),
        other.reshape(8, 2, 8, 16, 128),
        top,
        ((halves.astype(f32) - 1.0) * (1000000000.0 * log2e)).reshape(512, 1),
        end_in,
        end_in[:, 256:].T,
        end_out,
    )

    pieces = result.reshape(8, 2, 2, 8, 8, 128).transpose(3, 1, 2, 4, 0, 5).reshape(16, 128, 128)
    pieces = swap(pieces, same_c).reshape(8, 2, 2, 8, 2, 4, 128).transpose(3, 1, 2, 4, 0, 5, 6)
    return pieces.reshape(32, 64, 128)


def solution(mesh):
    parts = Mesh(mesh.devices.reshape(2, 4, 2, 4, 2), everyone)
    placed = P(("xl", "y", "core"), ("z", "xh"), None)
    in_specs = (placed,) + (P(),) * 9
    return jax.shard_map(body, mesh=parts, in_specs=in_specs, out_specs=placed, check_vma=False)
```

```python
import jax
import jax.numpy as jnp
from jax import lax
from jax.experimental import pallas as pl
from jax.experimental.pallas import tpu as pltpu
from jax.sharding import Mesh, PartitionSpec as P

everyone = ("xl", "y", "core", "z", "xh")
by_row = ("z", "xh", "core")
same_c = ("xl", "y", "core")
epsilon = 1e-05
bf16, f32 = jnp.bfloat16, jnp.float32
log2e = 1.4426950408889634
lowest = -3e38


def swap(pieces, axes):
    return lax.all_to_all(pieces, axes, 0, 0, tiled=True)


def layer_norm(values_in, axis=-1):
    average = jnp.mean(values_in, axis=axis, keepdims=True)
    centred = values_in - average
    variance = jnp.mean(centred * centred, axis=axis, keepdims=True)
    return centred * lax.rsqrt(variance + epsilon)


def dot(a, b, dims):
    return lax.dot_general(a, b, (dims, ((), ())), preferred_element_type=f32)


def nn(a, b):
    return dot(a, b, ((1,), (0,)))


def nt(a, b):
    return dot(a, b, ((1,), (1,)))


def head_lanes(rows):
    lanes = lax.broadcasted_iota(jnp.int32, (rows, 128), 1)
    return [(lanes >= 32 * head) & (lanes < 32 * head + 32) for head in range(4)]


def terms_kernel(pair_ref, w_in_ref, mask_ref, left_ref, right_ref, held_ref):
    for step in range(8):
        rows = [(place % 8) * 4 + ah * 2 + place // 8 for place in (2 * step, 2 * step + 1) for ah in range(2)]
        tokens = jnp.concatenate([pair_ref[row] for row in rows], axis=0).astype(f32)
        terms = dot(w_in_ref[...], layer_norm(tokens).astype(bf16), ((0,), (1,)))
        for side in range(2):
            at = side * 256
            kept = jax.nn.sigmoid(terms[at : at + 128]) * terms[at + 128 : at + 256] * mask_ref[step : step + 1, :]
            for odd in range(2):
                held_ref[side, pl.ds(2 * step + odd, 128, stride=16), :] = kept[:, odd * 128 : odd * 128 + 128]
    left_ref[...] = held_ref[0].astype(bf16).reshape(128, 16, 128)
    right_ref[...] = held_ref[1].astype(bf16).reshape(128, 16, 128)


def triangle_kernel(both_ref, out_ref, left_ref, right_ref):
    at = lax.broadcasted_iota(jnp.int32, (256, 256), 0)
    to = lax.broadcasted_iota(jnp.int32, (256, 256), 1)
    lanes = (at == to // 64 % 2 * 128 + to // 128 * 64 + to % 64).astype(f32).astype(bf16)
    for side, kept_ref in ((0, left_ref), (1, right_ref)):
        for pair_at in range(4):
            taken = [
                both_ref[:, :, pair_at * 2 + odd, side * 16 : side * 16 + 16, :].reshape(256, 128) for odd in range(2)
            ]
            moved = nn(jnp.concatenate(taken, axis=1), lanes).astype(bf16)
            for pi in range(2):
                kept_ref[pi, :, pair_at * 128 : pair_at * 128 + 128] = moved[:, pi * 128 : pi * 128 + 128]
    place = to * 0 + at // 8 % 8 * 32 + at // 128 * 16 + at // 64 % 2 * 8 + at % 8
    order = (to == place).astype(f32).astype(bf16)
    right = [nn(order, right_ref[pi]).astype(bf16) for pi in range(2)]
    right = jnp.concatenate([right[pi][half * 128 : half * 128 + 128] for half in range(2) for pi in range(2)], axis=0)
    place = to * 0 + at // 2 % 2 * 128 + at // 64 * 32 + at // 4 % 2 * 16 + at % 2 * 8 + at // 8 % 8
    order = (to == place).astype(f32).astype(bf16)
    for block in range(2):
        taken = jnp.concatenate([left_ref[pi, block * 128 : block * 128 + 128, :] for pi in range(2)], axis=0)
        left = nn(order, taken).astype(bf16)
        combined = nt(left, right)
        for q in range(4):
            for half in range(2):
                piece = combined[q * 64 : q * 64 + 64, half * 256 : half * 256 + 256].reshape(8, 8, 256)
                piece = jnp.concatenate([piece[:, :, :128], piece[:, :, 128:]], axis=1)
                out_ref[block * 4 + q, half] = piece.astype(bf16)


def mix_kernel(combined_ref, pair_ref, gate_ref, w_ref, one_ref, normed_ref, held_ref):
    held_ref[...] = layer_norm(combined_ref[...].astype(f32), 0).reshape(2048, 128)
    for step in range(8):
        mixed = [held_ref[pl.ds(2 * step + odd, 128, stride=16), :] for odd in range(2)]
        update = dot(jnp.concatenate(mixed, axis=1).astype(bf16), w_ref[...], ((0,), (0,)))
        rows = slice(2 * step, 2 * step + 2)
        pair = pair_ref[rows].reshape(256, 128).astype(f32)
        one = (pair + gate_ref[rows].reshape(256, 128) * update).astype(bf16)
        one_ref[rows] = one.reshape(2, 128, 128)
        normed_ref[rows] = layer_norm(one.astype(f32)).astype(bf16).reshape(2, 128, 128)


def bias_kernel(own_ref, other_ref, w_ref, mask_ref, out_ref, held_ref):
    sides = [nt(w_ref[...], side[...].reshape(2048, 128)) for side in (own_ref, other_ref)]
    for row in range(8):
        parts = [side[:, ah * 1024 + row * 128 : ah * 1024 + row * 128 + 128] for side in sides for ah in range(2)]
        largest, top = parts[0], jnp.full((8, 128), lowest, f32)
        for place, part in enumerate(parts):
            largest = jnp.maximum(largest, part)
            top = jnp.maximum(top, jnp.where(mask_ref[:, place * 128 : place * 128 + 128] > 0, part, lowest))
        top = jnp.max(top, axis=1, keepdims=True)
        top = jnp.where(top > -1e38, top, jnp.max(largest, axis=1, keepdims=True))
        for ah in range(2):
            at = ah * 16 + row % 4 * 4
            held_ref[row // 4, at : at + 4, :] = (parts[ah] - top)[0:4]
    out_ref[...] = jnp.broadcast_to(held_ref[...].astype(bf16)[None, :, None], (8, 2, 8, 32, 128))


def start_kernel(core_ref, kept_ref, own_ref, other_ref, rest_ref, mask_ref, w_in_ref, w_out_ref, pair_ref, next_ref,
                 out_ref, extra_ref, bias_ref, after_ref):
    core = core_ref[0]
    to = lax.broadcasted_iota(jnp.int32, (256, 256), 0)
    place = (to // 8 % 2 * 8 + to % 8) * 16 + (to // 16 % 4) * 4 + to // 64
    order = (lax.broadcasted_iota(jnp.int32, (256, 256), 1) == place).astype(f32).astype(bf16)
    for half in range(2):
        source = core if half == 0 else 1 - core
        mask_bias = mask_ref[:, half * 256 : half * 256 + 256]
        for block in range(4):
            taken = [
                rest_ref[block * 2 : block * 2 + 2, source, :, part * 16 : part * 16 + 16, :].reshape(256, 128)
                for part in range(2)
            ]
            placed = nn(order, jnp.concatenate(taken, axis=1)) * log2e + mask_bias
            for head in range(4):
                for part in range(4):
                    at = head * 64 + part * 16
                    bias_ref[head, part * 64 + block * 16 : part * 64 + block * 16 + 16, half * 256 : half * 256 + 256] = (
                        placed[at : at + 16]
                    )
    heads = head_lanes(256)
    ones = jnp.ones((512, 128), bf16)

    def two_rows(step, carry):
        rows = pl.ds(step * 4, 4)
        projected = nn(own_ref[:, rows].reshape(1024, 128), w_in_ref[...])
        projected_other = nn(other_ref[:, rows].reshape(1024, 128), w_in_ref[:, 128:384])
        gated = []
        for row in range(4):
            one, two = (
                jnp.concatenate([whole[row * 128 : row * 128 + 128], whole[512 + row * 128 : 640 + row * 128]], axis=0)
                for whole in (projected, projected_other)
            )
            query = (one[:, :128] * (32 ** (-0.5) * log2e)).astype(bf16)
            keys = jnp.concatenate([one[:, 128:256], two[:, :128]], axis=0).astype(bf16)
            values = jnp.concatenate([one[:, 256:384], two[:, 128:]], axis=0).astype(bf16)
            values = jnp.concatenate([values, ones], axis=1)
            queries = jnp.concatenate([jnp.where(lanes, query, jnp.zeros_like(query)) for lanes in heads], axis=0)
            scores = nt(queries, keys)
            attended = jnp.zeros((256, 128), f32)
            for head in range(4):
                part = scores[head * 256 : head * 256 + 256] + bias_ref[head]
                weights = jnp.exp2(part - jnp.max(part, axis=1, keepdims=True)).astype(bf16)
                summed = nn(weights, values)
                attended = jnp.where(heads[head], summed[:, :128] / summed[:, 128:], attended)
            gated.append((attended * jax.nn.sigmoid(one[:, 384:])).astype(bf16))
        update = nn(jnp.concatenate(gated, axis=0), w_out_ref[...])
        for row in range(4):
            at = step * 4 + row
            pair = pair_ref[:, at].reshape(256, 128).astype(f32)
            out_ref[:, at] = (pair + update[row * 256 : row * 256 + 256]).astype(bf16).reshape(2, 128, 128)
        return carry

    lax.fori_loop(0, 2, two_rows, 0)
    for row in range(8):
        normed = layer_norm(out_ref[:, row].reshape(256, 128).astype(f32)).astype(bf16)
        after_ref[row] = nt(next_ref[...], normed)
    largest, top = after_ref[0], jnp.full((8, 256), lowest, f32)
    for row in range(8):
        largest = jnp.maximum(largest, after_ref[row])
        top = jnp.maximum(top, jnp.where(kept_ref[row] > 0, after_ref[row], lowest))
    top = jnp.where(top > -1e38, top, largest).astype(bf16).astype(f32)
    for ah in range(2):
        extra_ref[ah, 32:40, :] = top[:, ah * 128 : ah * 128 + 128]
        for row in range(8):
            remains = after_ref[row] - top
            extra_ref[ah, row * 4 : row * 4 + 4, :] = remains[0:4, ah * 128 : ah * 128 + 128]


def end_kernel(core_ref, pieces_ref, other_ref, top_ref, mask_ref, w_in_ref, w_turned_ref, w_out_ref, out_ref, bias_ref,
               own_ref, both_ref):
    core = core_ref[0]
    to = lax.broadcasted_iota(jnp.int32, (256, 256), 0)
    key = to // 16 % 2 * 4 + to // 32 % 2 * 2 + to // 8 % 2
    place = to % 8 * 32 + key * 4 + to // 64
    order = (lax.broadcasted_iota(jnp.int32, (256, 256), 1) == place).astype(f32).astype(bf16)
    to = lax.broadcasted_iota(jnp.int32, (256, 64), 0)
    order_top = (lax.broadcasted_iota(jnp.int32, (256, 64), 1) == to % 8 * 8 + to // 64).astype(f32).astype(bf16)
    for block in range(8):
        rest = jnp.concatenate([pieces_ref[block, t, :, 16:48, :].reshape(256, 128) for t in range(2)], axis=1)
        top = jnp.concatenate([top_ref[block, t].reshape(64, 128).astype(bf16) for t in range(2)], axis=1)
        placed = (nn(order, rest) + nn(order_top, top)) * log2e
        for ah in range(2):
            half = core if ah == 0 else 1 - core
            for part in range(4):
                rows = pl.ds(pl.multiple_of(half * 256 + part * 64 + block * 8, 8), 8)
                mask_bias = mask_ref[rows, :]
                for head in range(4):
                    at = head * 64 + ah * 32 + part * 8
                    bias_ref[head, rows, :] = placed[at : at + 8] + mask_bias
    for block in range(8):
        for t in range(2):
            rows = slice(block * 128, block * 128 + 128)
            own_ref[t, rows, :] = pieces_ref[block, t, :, 0:16, :].astype(f32).reshape(128, 128)
            both_ref[t, rows, :] = other_ref[block, t].astype(f32).reshape(128, 128)
    heads = head_lanes(512)
    ones = jnp.ones((16, 512), bf16)

    def taken(from_ref, column):
        return jnp.concatenate(
            [from_ref[column // 4, pl.ds(column % 4 * 4 + part, 64, stride=16), :] for part in range(4)], axis=0
        )

    def two_columns(step, carry):
        pair = jnp.concatenate([taken(own_ref, step * 4 + place) for place in range(4)], axis=0)
        other = jnp.concatenate([taken(both_ref, step * 4 + place) for place in range(4)], axis=0)
        own, other = layer_norm(pair).astype(bf16), layer_norm(other).astype(bf16)
        first = nn(own, w_in_ref[:, :256])
        query = (first[:, :128] * (32 ** (-0.5) * log2e)).astype(bf16)
        keys_own, keys_other = first[:, 128:].astype(bf16), nn(other, w_in_ref[:, 128:256]).astype(bf16)
        turned = nt(w_turned_ref[...], own)
        values_own, values_other = turned[:128].astype(bf16), nt(w_turned_ref[:128], other).astype(bf16)
        gate = jax.nn.sigmoid(turned[128:])
        gated = []
        for place in range(4):
            at = slice(place * 256, place * 256 + 256)
            keys = jnp.concatenate([keys_own[at], keys_other[at]], axis=0)
            values = jnp.concatenate([values_own[:, at], values_other[:, at]], axis=1)
            stacked = jnp.concatenate([jnp.where(lanes, keys, jnp.zeros_like(keys)) for lanes in heads], axis=0)
            scores = nt(stacked, query[at])
            attended = []
            for head in range(4):
                part = scores[head * 512 : head * 512 + 512] + bias_ref[head]
                weights = jnp.exp2(part - jnp.max(part, axis=0, keepdims=True)).astype(bf16)
                summed = nn(jnp.concatenate([values[head * 32 : head * 32 + 32], ones], axis=0), weights)
                attended.append(summed[:32] / summed[32:33])
            gated.append(jnp.concatenate(attended, axis=0))
        gated = (jnp.concatenate(gated, axis=1) * gate).astype(bf16)
        result = (pair + dot(gated, w_out_ref[...], ((0,), (0,)))).astype(bf16)
        out_ref[pl.ds(step * 4, 4)] = result.reshape(4, 256, 128)
        return carry

    lax.fori_loop(0, 2, two_columns, 0)


def call(kernel, in_kinds, outs, scratch, flops):
    spaces = {"s": pltpu.SMEM, "v": pltpu.VMEM}
    return pl.pallas_call(
        kernel,
        out_shape=outs,
        in_specs=[pl.BlockSpec(memory_space=spaces[kind]) for kind in in_kinds],
        out_specs=jax.tree.map(lambda _: pl.BlockSpec(memory_space=pltpu.VMEM), outs),
        scratch_shapes=scratch,
        compiler_params=pltpu.CompilerParams(vmem_limit_bytes=40 * 2**20),
        cost_estimate=pl.CostEstimate(flops=flops, bytes_accessed=4 * 2**20, transcendentals=4 * 2**20),
    )


def body(pair, mask, tri_in, tri_out, start_in, start_bias, start_out, end_in, end_bias, end_out):
    q = lax.axis_index(("xl", "y"))
    core = lax.axis_index("core")
    c = lax.axis_index(("z", "xh"))
    maskf = mask.astype(f32)

    rows = swap(pair.reshape(16, 128, 128), by_row).reshape(8, 2, 2, 2, 32, 128)

    row_mask = lax.dynamic_slice_in_dim(maskf, (2 * q + core) * 32, 32)
    col_mask = lax.dynamic_slice_in_dim(maskf, c * 64, 64)
    pair_mask = (row_mask.reshape(8, 2, 2).transpose(2, 0, 1).reshape(16, 2, 1) * col_mask).reshape(8, 256)
    both = call(
        terms_kernel,
        "vvv",
        (jax.ShapeDtypeStruct((128, 16, 128), bf16),) * 2,
        [pltpu.VMEM((2, 2048, 128), f32)],
        3 * 10**8,
    )(pair, tri_in[:, :512], pair_mask)
    both = jnp.concatenate(both, axis=1)
    both, rows = lax.optimization_barrier((both, rows))
    both = swap(both, everyone).reshape(8, 2, 8, 32, 128)
    kept = lax.dynamic_index_in_dim(rows, core, 3, False)
    given = lax.ppermute(lax.dynamic_index_in_dim(rows, 1 - core, 3, False), "core", [(0, 1), (1, 0)])
    rows = jnp.stack([jnp.where(core == 0, kept, given), jnp.where(core == 0, given, kept)])
    rows = rows.reshape(2, 8, 2, 2, 8, 2, 2, 128).transpose(5, 2, 0, 3, 6, 1, 4, 7)
    pair_rows = rows.reshape(2048, 128)
    pieces = call(
        triangle_kernel,
        "v",
        jax.ShapeDtypeStruct((8, 2, 8, 16, 128), bf16),
        [pltpu.VMEM((2, 256, 512), bf16)] * 2,
        3 * 10**8,
    )(both)
    combined = swap(pieces.reshape(128, 16, 128), everyone)

    normed_rows = layer_norm(pair_rows.astype(f32)).astype(bf16)
    gate = jax.nn.sigmoid(dot(normed_rows, tri_in[:, 512:], ((1,), (0,))))
    pair_one, normed = call(
        mix_kernel,
        "vvvv",
        (jax.ShapeDtypeStruct((16, 128, 128), bf16),) * 2,
        [pltpu.VMEM((2048, 128), f32)],
        2 * 10**8,
    )(combined, pair_rows.reshape(16, 128, 128), gate.reshape(16, 128, 128), tri_out)

    other = lax.ppermute(normed, "core", [(0, 1), (1, 0)])
    halves = mask.reshape(8, 2, 8, 2, 2).transpose(1, 3, 4, 0, 2).reshape(2, 256)
    halves = jnp.concatenate([lax.dynamic_slice_in_dim(halves, place, 1) for place in (core, 1 - core)], axis=1)
    pieces = call(
        bias_kernel,
        "vvvv",
        jax.ShapeDtypeStruct((8, 2, 8, 32, 128), bf16),
        [pltpu.VMEM((2, 32, 128), f32)],
        10**8,
    )(
        normed.reshape(2, 8, 128, 128),
        other.reshape(2, 8, 128, 128),
        jnp.pad(start_bias.T, ((0, 4), (0, 0))),
        halves.astype(f32),
    )
    rest = swap(pieces.reshape(128, 32, 128), everyone).reshape(8, 2, 8, 32, 128)
    own_rows = lax.dynamic_index_in_dim(mask.reshape(8, 2, 8, 4), c, 2, False)
    own_rows = lax.dynamic_index_in_dim(own_rows, q, 0, False).reshape(8)
    here = core.astype(jnp.int32).reshape(1)
    next_bias = jnp.pad(end_bias.T, ((0, 4), (0, 0)))
    pair_two, extra = call(
        start_kernel,
        "ssvvvvvvvv",
        (jax.ShapeDtypeStruct((2, 8, 128, 128), bf16), jax.ShapeDtypeStruct((2, 40, 128), f32)),
        [pltpu.VMEM((4, 256, 512), f32), pltpu.VMEM((8, 8, 256), f32)],
        3 * 10**9,
    )(
        here,
        own_rows,
        normed.reshape(2, 8, 128, 128),
        other.reshape(2, 8, 128, 128),
        rest,
        (halves.astype(f32) - 1.0) * (1000000000.0 * log2e),
        start_in,
        start_out,
        pair_one.reshape(2, 8, 128, 128),
        next_bias,
    )

    extra = jnp.broadcast_to(extra.astype(bf16)[None, :, None], (8, 2, 8, 40, 128)).reshape(128, 40, 128)
    pieces = pair_two.reshape(2, 2, 2, 2, 2, 8, 8, 128).transpose(6, 2, 5, 0, 4, 1, 3, 7).reshape(128, 16, 128)
    pieces = swap(jnp.concatenate([pieces, extra], axis=1), everyone)
    other = lax.ppermute(pieces[:, :16], "core", [(0, 1), (1, 0)])
    top = pieces[:, 48:].astype(f32).reshape(8, 2, 8, 8, 128)

    halves = mask.reshape(8, 2, 8, 2, 2).transpose(3, 1, 4, 0, 2).reshape(2, 256)
    halves = jnp.concatenate([lax.dynamic_slice_in_dim(halves, place, 1) for place in (core, 1 - core)], axis=1)
    result = call(
        end_kernel,
        "svvvvvvv",
        jax.ShapeDtypeStruct((8, 256, 128), bf16),
        [pltpu.VMEM((4, 512, 256), f32)] + [pltpu.VMEM((2, 1024, 128), f32)] * 2,
        3 * 10**9,
    )(
        here,
        pieces.reshape(8, 2, 8, 56, 128),
        other.reshape(8, 2, 8, 16, 128),
        top,
        ((halves.astype(f32) - 1.0) * (1000000000.0 * log2e)).reshape(512, 1),
        end_in,
        end_in[:, 256:].T,
        end_out,
    )

    pieces = result.reshape(8, 2, 2, 8, 8, 128).transpose(3, 1, 2, 4, 0, 5).reshape(16, 128, 128)
    pieces = swap(pieces, same_c).reshape(8, 2, 2, 8, 2, 4, 128).transpose(3, 1, 2, 4, 0, 5, 6)
    return pieces.reshape(32, 64, 128)


def solution(mesh):
    parts = Mesh(mesh.devices.reshape(2, 4, 2, 4, 2), everyone)
    placed = P(("xl", "y", "core"), ("z", "xh"), None)
    in_specs = (placed,) + (P(),) * 9
    return jax.shard_map(body, mesh=parts, in_specs=in_specs, out_specs=placed, check_vma=False)
```

```python
import jax
import jax.numpy as jnp
from jax import lax
from jax.experimental import pallas as pl
from jax.experimental.pallas import tpu as pltpu
from jax.sharding import Mesh, PartitionSpec as P

everyone = ("xl", "y", "core", "z", "xh")
by_row = ("z", "xh", "core")
same_c = ("xl", "y", "core")
epsilon = 1e-05
bf16, f32 = jnp.bfloat16, jnp.float32
log2e = 1.4426950408889634
lowest = -3e38


def swap(pieces, axes):
    return lax.all_to_all(pieces, axes, 0, 0, tiled=True)


def layer_norm(values_in, axis=-1):
    average = jnp.mean(values_in, axis=axis, keepdims=True)
    centred = values_in - average
    variance = jnp.mean(centred * centred, axis=axis, keepdims=True)
    return centred * lax.rsqrt(variance + epsilon)


def dot(a, b, dims):
    return lax.dot_general(a, b, (dims, ((), ())), preferred_element_type=f32)


def nn(a, b):
    return dot(a, b, ((1,), (0,)))


def nt(a, b):
    return dot(a, b, ((1,), (1,)))


def head_lanes(rows):
    lanes = lax.broadcasted_iota(jnp.int32, (rows, 128), 1)
    return [(lanes >= 32 * head) & (lanes < 32 * head + 32) for head in range(4)]


def terms_kernel(pair_ref, w_in_ref, mask_ref, left_ref, right_ref, held_ref):
    for step in range(8):
        rows = [(place % 8) * 4 + ah * 2 + place // 8 for place in (2 * step, 2 * step + 1) for ah in range(2)]
        tokens = jnp.concatenate([pair_ref[row] for row in rows], axis=0).astype(f32)
        terms = dot(w_in_ref[...], layer_norm(tokens).astype(bf16), ((0,), (1,)))
        for side in range(2):
            at = side * 256
            kept = jax.nn.sigmoid(terms[at : at + 128]) * terms[at + 128 : at + 256] * mask_ref[step : step + 1, :]
            for odd in range(2):
                held_ref[side, pl.ds(2 * step + odd, 128, stride=16), :] = kept[:, odd * 128 : odd * 128 + 128]
    left_ref[...] = held_ref[0].astype(bf16).reshape(128, 16, 128)
    right_ref[...] = held_ref[1].astype(bf16).reshape(128, 16, 128)


def triangle_kernel(both_ref, out_ref, left_ref, right_ref):
    at = lax.broadcasted_iota(jnp.int32, (256, 256), 0)
    to = lax.broadcasted_iota(jnp.int32, (256, 256), 1)
    lanes = (at == to // 64 % 2 * 128 + to // 128 * 64 + to % 64).astype(f32).astype(bf16)
    for side, kept_ref in ((0, left_ref), (1, right_ref)):
        for pair_at in range(4):
            taken = [
                both_ref[:, :, pair_at * 2 + odd, side * 16 : side * 16 + 16, :].reshape(256, 128) for odd in range(2)
            ]
            moved = nn(jnp.concatenate(taken, axis=1), lanes).astype(bf16)
            for pi in range(2):
                kept_ref[pi, :, pair_at * 128 : pair_at * 128 + 128] = moved[:, pi * 128 : pi * 128 + 128]
    place = to * 0 + at // 8 % 8 * 32 + at // 128 * 16 + at // 64 % 2 * 8 + at % 8
    order = (to == place).astype(f32).astype(bf16)
    right = [nn(order, right_ref[pi]).astype(bf16) for pi in range(2)]
    right = jnp.concatenate([right[pi][half * 128 : half * 128 + 128] for half in range(2) for pi in range(2)], axis=0)
    place = to * 0 + at // 2 % 2 * 128 + at // 64 * 32 + at // 4 % 2 * 16 + at % 2 * 8 + at // 8 % 8
    order = (to == place).astype(f32).astype(bf16)
    for block in range(2):
        taken = jnp.concatenate([left_ref[pi, block * 128 : block * 128 + 128, :] for pi in range(2)], axis=0)
        left = nn(order, taken).astype(bf16)
        combined = nt(left, right)
        for q in range(4):
            for half in range(2):
                piece = combined[q * 64 : q * 64 + 64, half * 256 : half * 256 + 256].reshape(8, 8, 256)
                piece = jnp.concatenate([piece[:, :, :128], piece[:, :, 128:]], axis=1)
                out_ref[block * 4 + q, half] = piece.astype(bf16)


def mix_kernel(combined_ref, pair_ref, gate_ref, w_ref, one_ref, normed_ref, held_ref):
    held_ref[...] = layer_norm(combined_ref[...].astype(f32), 0).reshape(2048, 128)
    for step in range(8):
        mixed = [held_ref[pl.ds(2 * step + odd, 128, stride=16), :] for odd in range(2)]
        update = dot(jnp.concatenate(mixed, axis=1).astype(bf16), w_ref[...], ((0,), (0,)))
        rows = slice(2 * step, 2 * step + 2)
        pair = pair_ref[rows].reshape(256, 128).astype(f32)
        one = (pair + gate_ref[rows].reshape(256, 128) * update).astype(bf16)
        one_ref[rows] = one.reshape(2, 128, 128)
        normed_ref[rows] = layer_norm(one.astype(f32)).astype(bf16).reshape(2, 128, 128)


def bias_kernel(own_ref, other_ref, w_ref, mask_ref, out_ref, held_ref):
    sides = [nt(w_ref[...], side[...].reshape(2048, 128)) for side in (own_ref, other_ref)]
    for row in range(8):
        parts = [side[:, ah * 1024 + row * 128 : ah * 1024 + row * 128 + 128] for side in sides for ah in range(2)]
        largest, top = parts[0], jnp.full((8, 128), lowest, f32)
        for place, part in enumerate(parts):
            largest = jnp.maximum(largest, part)
            top = jnp.maximum(top, jnp.where(mask_ref[:, place * 128 : place * 128 + 128] > 0, part, lowest))
        top = jnp.max(top, axis=1, keepdims=True)
        top = jnp.where(top > -1e38, top, jnp.max(largest, axis=1, keepdims=True))
        for ah in range(2):
            at = ah * 16 + row % 4 * 4
            held_ref[row // 4, at : at + 4, :] = (parts[ah] - top)[0:4]
    out_ref[...] = jnp.broadcast_to(held_ref[...].astype(bf16)[None, :, None], (8, 2, 8, 32, 128))


def start_kernel(core_ref, kept_ref, own_ref, other_ref, rest_ref, mask_ref, w_in_ref, w_out_ref, pair_ref, next_ref,
                 out_ref, extra_ref, bias_ref, after_ref):
    core = core_ref[0]
    to = lax.broadcasted_iota(jnp.int32, (256, 256), 0)
    place = (to // 8 % 2 * 8 + to % 8) * 16 + (to // 16 % 4) * 4 + to // 64
    order = (lax.broadcasted_iota(jnp.int32, (256, 256), 1) == place).astype(f32).astype(bf16)
    for half in range(2):
        source = core if half == 0 else 1 - core
        mask_bias = mask_ref[:, half * 256 : half * 256 + 256]
        for block in range(4):
            taken = [
                rest_ref[block * 2 : block * 2 + 2, source, :, part * 16 : part * 16 + 16, :].reshape(256, 128)
                for part in range(2)
            ]
            placed = nn(order, jnp.concatenate(taken, axis=1)) * log2e + mask_bias
            for head in range(4):
                for part in range(4):
                    at = head * 64 + part * 16
                    bias_ref[head, part * 64 + block * 16 : part * 64 + block * 16 + 16, half * 256 : half * 256 + 256] = (
                        placed[at : at + 16]
                    )
    heads = head_lanes(256)
    ones = jnp.ones((512, 128), bf16)

    def two_rows(step, carry):
        rows = pl.ds(step * 8, 8)
        projected = nn(own_ref[:, rows].reshape(2048, 128), w_in_ref[...])
        projected_other = nn(other_ref[:, rows].reshape(2048, 128), w_in_ref[:, 128:384])
        gated = []
        for row in range(8):
            one, two = (
                jnp.concatenate([whole[row * 128 : row * 128 + 128], whole[1024 + row * 128 : 1152 + row * 128]], axis=0)
                for whole in (projected, projected_other)
            )
            query = (one[:, :128] * (32 ** (-0.5) * log2e)).astype(bf16)
            keys = jnp.concatenate([one[:, 128:256], two[:, :128]], axis=0).astype(bf16)
            values = jnp.concatenate([one[:, 256:384], two[:, 128:]], axis=0).astype(bf16)
            values = jnp.concatenate([values, ones], axis=1)
            queries = jnp.concatenate([jnp.where(lanes, query, jnp.zeros_like(query)) for lanes in heads], axis=0)
            scores = nt(queries, keys)
            attended = jnp.zeros((256, 128), f32)
            for head in range(4):
                part = scores[head * 256 : head * 256 + 256] + bias_ref[head]
                weights = jnp.exp2(part - jnp.max(part, axis=1, keepdims=True)).astype(bf16)
                summed = nn(weights, values)
                attended = jnp.where(heads[head], summed[:, :128] / summed[:, 128:], attended)
            gated.append((attended * jax.nn.sigmoid(one[:, 384:])).astype(bf16))
        update = nn(jnp.concatenate(gated, axis=0), w_out_ref[...])
        for row in range(8):
            at = step * 8 + row
            pair = pair_ref[:, at].reshape(256, 128).astype(f32)
            out_ref[:, at] = (pair + update[row * 256 : row * 256 + 256]).astype(bf16).reshape(2, 128, 128)
        return carry

    lax.fori_loop(0, 1, two_rows, 0)
    for row in range(8):
        normed = layer_norm(out_ref[:, row].reshape(256, 128).astype(f32)).astype(bf16)
        after_ref[row] = nt(next_ref[...], normed)
    largest, top = after_ref[0], jnp.full((8, 256), lowest, f32)
    for row in range(8):
        largest = jnp.maximum(largest, after_ref[row])
        top = jnp.maximum(top, jnp.where(kept_ref[row] > 0, after_ref[row], lowest))
    top = jnp.where(top > -1e38, top, largest).astype(bf16).astype(f32)
    for ah in range(2):
        extra_ref[ah, 32:40, :] = top[:, ah * 128 : ah * 128 + 128]
        for row in range(8):
            remains = after_ref[row] - top
            extra_ref[ah, row * 4 : row * 4 + 4, :] = remains[0:4, ah * 128 : ah * 128 + 128]


def end_kernel(core_ref, pieces_ref, other_ref, top_ref, mask_ref, w_in_ref, w_turned_ref, w_out_ref, out_ref, bias_ref,
               own_ref, both_ref):
    core = core_ref[0]
    to = lax.broadcasted_iota(jnp.int32, (256, 256), 0)
    key = to // 16 % 2 * 4 + to // 32 % 2 * 2 + to // 8 % 2
    place = to % 8 * 32 + key * 4 + to // 64
    order = (lax.broadcasted_iota(jnp.int32, (256, 256), 1) == place).astype(f32).astype(bf16)
    to = lax.broadcasted_iota(jnp.int32, (256, 64), 0)
    order_top = (lax.broadcasted_iota(jnp.int32, (256, 64), 1) == to % 8 * 8 + to // 64).astype(f32).astype(bf16)
    for block in range(8):
        rest = jnp.concatenate([pieces_ref[block, t, :, 16:48, :].reshape(256, 128) for t in range(2)], axis=1)
        top = jnp.concatenate([top_ref[block, t].reshape(64, 128).astype(bf16) for t in range(2)], axis=1)
        placed = (nn(order, rest) + nn(order_top, top)) * log2e
        for ah in range(2):
            half = core if ah == 0 else 1 - core
            for part in range(4):
                rows = pl.ds(pl.multiple_of(half * 256 + part * 64 + block * 8, 8), 8)
                mask_bias = mask_ref[rows, :]
                for head in range(4):
                    at = head * 64 + ah * 32 + part * 8
                    bias_ref[head, rows, :] = placed[at : at + 8] + mask_bias
    for block in range(8):
        for t in range(2):
            rows = slice(block * 128, block * 128 + 128)
            own_ref[t, rows, :] = pieces_ref[block, t, :, 0:16, :].astype(f32).reshape(128, 128)
            both_ref[t, rows, :] = other_ref[block, t].astype(f32).reshape(128, 128)
    heads = head_lanes(512)
    ones = jnp.ones((16, 512), bf16)

    def taken(from_ref, column):
        return jnp.concatenate(
            [from_ref[column // 4, pl.ds(column % 4 * 4 + part, 64, stride=16), :] for part in range(4)], axis=0
        )

    def two_columns(step, carry):
        pair = jnp.concatenate([taken(own_ref, step * 8 + place) for place in range(8)], axis=0)
        other = jnp.concatenate([taken(both_ref, step * 8 + place) for place in range(8)], axis=0)
        own, other = layer_norm(pair).astype(bf16), layer_norm(other).astype(bf16)
        first = nn(own, w_in_ref[:, :256])
        query = (first[:, :128] * (32 ** (-0.5) * log2e)).astype(bf16)
        keys_own, keys_other = first[:, 128:].astype(bf16), nn(other, w_in_ref[:, 128:256]).astype(bf16)
        turned = nt(w_turned_ref[...], own)
        values_own, values_other = turned[:128].astype(bf16), nt(w_turned_ref[:128], other).astype(bf16)
        gate = jax.nn.sigmoid(turned[128:])
        gated = []
        for place in range(8):
            at = slice(place * 256, place * 256 + 256)
            keys = jnp.concatenate([keys_own[at], keys_other[at]], axis=0)
            values = jnp.concatenate([values_own[:, at], values_other[:, at]], axis=1)
            stacked = jnp.concatenate([jnp.where(lanes, keys, jnp.zeros_like(keys)) for lanes in heads], axis=0)
            scores = nt(stacked, query[at])
            attended = []
            for head in range(4):
                part = scores[head * 512 : head * 512 + 512] + bias_ref[head]
                weights = jnp.exp2(part - jnp.max(part, axis=0, keepdims=True)).astype(bf16)
                summed = nn(jnp.concatenate([values[head * 32 : head * 32 + 32], ones], axis=0), weights)
                attended.append(summed[:32] / summed[32:33])
            gated.append(jnp.concatenate(attended, axis=0))
        gated = (jnp.concatenate(gated, axis=1) * gate).astype(bf16)
        result = (pair + dot(gated, w_out_ref[...], ((0,), (0,)))).astype(bf16)
        out_ref[pl.ds(step * 8, 8)] = result.reshape(8, 256, 128)
        return carry

    lax.fori_loop(0, 1, two_columns, 0)


def call(kernel, in_kinds, outs, scratch, flops):
    spaces = {"s": pltpu.SMEM, "v": pltpu.VMEM}
    return pl.pallas_call(
        kernel,
        out_shape=outs,
        in_specs=[pl.BlockSpec(memory_space=spaces[kind]) for kind in in_kinds],
        out_specs=jax.tree.map(lambda _: pl.BlockSpec(memory_space=pltpu.VMEM), outs),
        scratch_shapes=scratch,
        compiler_params=pltpu.CompilerParams(vmem_limit_bytes=40 * 2**20),
        cost_estimate=pl.CostEstimate(flops=flops, bytes_accessed=4 * 2**20, transcendentals=4 * 2**20),
    )


def body(pair, mask, tri_in, tri_out, start_in, start_bias, start_out, end_in, end_bias, end_out):
    q = lax.axis_index(("xl", "y"))
    core = lax.axis_index("core")
    c = lax.axis_index(("z", "xh"))
    maskf = mask.astype(f32)

    rows = swap(pair.reshape(16, 128, 128), by_row).reshape(8, 2, 2, 2, 32, 128)

    row_mask = lax.dynamic_slice_in_dim(maskf, (2 * q + core) * 32, 32)
    col_mask = lax.dynamic_slice_in_dim(maskf, c * 64, 64)
    pair_mask = (row_mask.reshape(8, 2, 2).transpose(2, 0, 1).reshape(16, 2, 1) * col_mask).reshape(8, 256)
    both = call(
        terms_kernel,
        "vvv",
        (jax.ShapeDtypeStruct((128, 16, 128), bf16),) * 2,
        [pltpu.VMEM((2, 2048, 128), f32)],
        3 * 10**8,
    )(pair, tri_in[:, :512], pair_mask)
    both = jnp.concatenate(both, axis=1)
    both, rows = lax.optimization_barrier((both, rows))
    both = swap(both, everyone).reshape(8, 2, 8, 32, 128)
    kept = lax.dynamic_index_in_dim(rows, core, 3, False)
    given = lax.ppermute(lax.dynamic_index_in_dim(rows, 1 - core, 3, False), "core", [(0, 1), (1, 0)])
    rows = jnp.stack([jnp.where(core == 0, kept, given), jnp.where(core == 0, given, kept)])
    rows = rows.reshape(2, 8, 2, 2, 8, 2, 2, 128).transpose(5, 2, 0, 3, 6, 1, 4, 7)
    pair_rows = rows.reshape(2048, 128)
    pieces = call(
        triangle_kernel,
        "v",
        jax.ShapeDtypeStruct((8, 2, 8, 16, 128), bf16),
        [pltpu.VMEM((2, 256, 512), bf16)] * 2,
        3 * 10**8,
    )(both)
    combined = swap(pieces.reshape(128, 16, 128), everyone)

    normed_rows = layer_norm(pair_rows.astype(f32)).astype(bf16)
    gate = jax.nn.sigmoid(dot(normed_rows, tri_in[:, 512:], ((1,), (0,))))
    pair_one, normed = call(
        mix_kernel,
        "vvvv",
        (jax.ShapeDtypeStruct((16, 128, 128), bf16),) * 2,
        [pltpu.VMEM((2048, 128), f32)],
        2 * 10**8,
    )(combined, pair_rows.reshape(16, 128, 128), gate.reshape(16, 128, 128), tri_out)

    other = lax.ppermute(normed, "core", [(0, 1), (1, 0)])
    halves = mask.reshape(8, 2, 8, 2, 2).transpose(1, 3, 4, 0, 2).reshape(2, 256)
    halves = jnp.concatenate([lax.dynamic_slice_in_dim(halves, place, 1) for place in (core, 1 - core)], axis=1)
    pieces = call(
        bias_kernel,
        "vvvv",
        jax.ShapeDtypeStruct((8, 2, 8, 32, 128), bf16),
        [pltpu.VMEM((2, 32, 128), f32)],
        10**8,
    )(
        normed.reshape(2, 8, 128, 128),
        other.reshape(2, 8, 128, 128),
        jnp.pad(start_bias.T, ((0, 4), (0, 0))),
        halves.astype(f32),
    )
    rest = swap(pieces.reshape(128, 32, 128), everyone).reshape(8, 2, 8, 32, 128)
    own_rows = lax.dynamic_index_in_dim(mask.reshape(8, 2, 8, 4), c, 2, False)
    own_rows = lax.dynamic_index_in_dim(own_rows, q, 0, False).reshape(8)
    here = core.astype(jnp.int32).reshape(1)
    next_bias = jnp.pad(end_bias.T, ((0, 4), (0, 0)))
    pair_two, extra = call(
        start_kernel,
        "ssvvvvvvvv",
        (jax.ShapeDtypeStruct((2, 8, 128, 128), bf16), jax.ShapeDtypeStruct((2, 40, 128), f32)),
        [pltpu.VMEM((4, 256, 512), f32), pltpu.VMEM((8, 8, 256), f32)],
        3 * 10**9,
    )(
        here,
        own_rows,
        normed.reshape(2, 8, 128, 128),
        other.reshape(2, 8, 128, 128),
        rest,
        (halves.astype(f32) - 1.0) * (1000000000.0 * log2e),
        start_in,
        start_out,
        pair_one.reshape(2, 8, 128, 128),
        next_bias,
    )

    extra = jnp.broadcast_to(extra.astype(bf16)[None, :, None], (8, 2, 8, 40, 128)).reshape(128, 40, 128)
    pieces = pair_two.reshape(2, 2, 2, 2, 2, 8, 8, 128).transpose(6, 2, 5, 0, 4, 1, 3, 7).reshape(128, 16, 128)
    pieces = swap(jnp.concatenate([pieces, extra], axis=1), everyone)
    other = lax.ppermute(pieces[:, :16], "core", [(0, 1), (1, 0)])
    top = pieces[:, 48:].astype(f32).reshape(8, 2, 8, 8, 128)

    halves = mask.reshape(8, 2, 8, 2, 2).transpose(3, 1, 4, 0, 2).reshape(2, 256)
    halves = jnp.concatenate([lax.dynamic_slice_in_dim(halves, place, 1) for place in (core, 1 - core)], axis=1)
    result = call(
        end_kernel,
        "svvvvvvv",
        jax.ShapeDtypeStruct((8, 256, 128), bf16),
        [pltpu.VMEM((4, 512, 256), f32)] + [pltpu.VMEM((2, 1024, 128), f32)] * 2,
        3 * 10**9,
    )(
        here,
        pieces.reshape(8, 2, 8, 56, 128),
        other.reshape(8, 2, 8, 16, 128),
        top,
        ((halves.astype(f32) - 1.0) * (1000000000.0 * log2e)).reshape(512, 1),
        end_in,
        end_in[:, 256:].T,
        end_out,
    )

    pieces = result.reshape(8, 2, 2, 8, 8, 128).transpose(3, 1, 2, 4, 0, 5).reshape(16, 128, 128)
    pieces = swap(pieces, same_c).reshape(8, 2, 2, 8, 2, 4, 128).transpose(3, 1, 2, 4, 0, 5, 6)
    return pieces.reshape(32, 64, 128)


def solution(mesh):
    parts = Mesh(mesh.devices.reshape(2, 4, 2, 4, 2), everyone)
    placed = P(("xl", "y", "core"), ("z", "xh"), None)
    in_specs = (placed,) + (P(),) * 9
    return jax.shard_map(body, mesh=parts, in_specs=in_specs, out_specs=placed, check_vma=False)
```

```python
import jax
import jax.numpy as jnp
from jax import lax
from jax.experimental import pallas as pl
from jax.experimental.pallas import tpu as pltpu
from jax.sharding import Mesh, PartitionSpec as P

everyone = ("xl", "y", "core", "z", "xh")
by_row = ("z", "xh", "core")
same_c = ("xl", "y", "core")
epsilon = 1e-05
bf16, f32 = jnp.bfloat16, jnp.float32
log2e = 1.4426950408889634
lowest = -3e38


def swap(pieces, axes):
    return lax.all_to_all(pieces, axes, 0, 0, tiled=True)


def layer_norm(values_in, axis=-1):
    average = jnp.mean(values_in, axis=axis, keepdims=True)
    centred = values_in - average
    variance = jnp.mean(centred * centred, axis=axis, keepdims=True)
    return centred * lax.rsqrt(variance + epsilon)


def dot(a, b, dims):
    return lax.dot_general(a, b, (dims, ((), ())), preferred_element_type=f32)


def nn(a, b):
    return dot(a, b, ((1,), (0,)))


def nt(a, b):
    return dot(a, b, ((1,), (1,)))


def head_lanes(rows):
    lanes = lax.broadcasted_iota(jnp.int32, (rows, 128), 1)
    return [(lanes >= 32 * head) & (lanes < 32 * head + 32) for head in range(4)]


def terms_kernel(pair_ref, w_in_ref, mask_ref, left_ref, right_ref, held_ref):
    for step in range(8):
        rows = [(place % 8) * 4 + ah * 2 + place // 8 for place in (2 * step, 2 * step + 1) for ah in range(2)]
        tokens = jnp.concatenate([pair_ref[row] for row in rows], axis=0).astype(f32)
        terms = dot(w_in_ref[...], layer_norm(tokens).astype(bf16), ((0,), (1,)))
        for side in range(2):
            at = side * 256
            kept = jax.nn.sigmoid(terms[at : at + 128]) * terms[at + 128 : at + 256] * mask_ref[step : step + 1, :]
            for odd in range(2):
                held_ref[side, pl.ds(2 * step + odd, 128, stride=16), :] = kept[:, odd * 128 : odd * 128 + 128]
    left_ref[...] = held_ref[0].astype(bf16).reshape(128, 16, 128)
    right_ref[...] = held_ref[1].astype(bf16).reshape(128, 16, 128)


def triangle_kernel(both_ref, out_ref, left_ref, right_ref):
    at = lax.broadcasted_iota(jnp.int32, (256, 256), 0)
    to = lax.broadcasted_iota(jnp.int32, (256, 256), 1)
    lanes = (at == to // 64 % 2 * 128 + to // 128 * 64 + to % 64).astype(f32).astype(bf16)
    for side, kept_ref in ((0, left_ref), (1, right_ref)):
        for pair_at in range(4):
            taken = [
                both_ref[:, :, pair_at * 2 + odd, side * 16 : side * 16 + 16, :].reshape(256, 128) for odd in range(2)
            ]
            moved = nn(jnp.concatenate(taken, axis=1), lanes).astype(bf16)
            for pi in range(2):
                kept_ref[pi, :, pair_at * 128 : pair_at * 128 + 128] = moved[:, pi * 128 : pi * 128 + 128]
    place = to * 0 + at // 8 % 8 * 32 + at // 128 * 16 + at // 64 % 2 * 8 + at % 8
    order = (to == place).astype(f32).astype(bf16)
    right = [nn(order, right_ref[pi]).astype(bf16) for pi in range(2)]
    right = jnp.concatenate([right[pi][half * 128 : half * 128 + 128] for half in range(2) for pi in range(2)], axis=0)
    place = to * 0 + at // 2 % 2 * 128 + at // 64 * 32 + at // 4 % 2 * 16 + at % 2 * 8 + at // 8 % 8
    order = (to == place).astype(f32).astype(bf16)
    for block in range(2):
        taken = jnp.concatenate([left_ref[pi, block * 128 : block * 128 + 128, :] for pi in range(2)], axis=0)
        left = nn(order, taken).astype(bf16)
        combined = nt(left, right)
        for q in range(4):
            for half in range(2):
                piece = combined[q * 64 : q * 64 + 64, half * 256 : half * 256 + 256].reshape(8, 8, 256)
                piece = jnp.concatenate([piece[:, :, :128], piece[:, :, 128:]], axis=1)
                out_ref[block * 4 + q, half] = piece.astype(bf16)


def mix_kernel(combined_ref, pair_ref, gate_ref, w_ref, one_ref, normed_ref, held_ref):
    held_ref[...] = layer_norm(combined_ref[...].astype(f32), 0).reshape(2048, 128)
    for step in range(8):
        mixed = [held_ref[pl.ds(2 * step + odd, 128, stride=16), :] for odd in range(2)]
        update = dot(jnp.concatenate(mixed, axis=1).astype(bf16), w_ref[...], ((0,), (0,)))
        rows = slice(2 * step, 2 * step + 2)
        pair = pair_ref[rows].reshape(256, 128).astype(f32)
        one = (pair + gate_ref[rows].reshape(256, 128) * update).astype(bf16)
        one_ref[rows] = one.reshape(2, 128, 128)
        normed_ref[rows] = layer_norm(one.astype(f32)).astype(bf16).reshape(2, 128, 128)


def bias_kernel(own_ref, other_ref, w_ref, mask_ref, out_ref, held_ref):
    sides = [nt(w_ref[...], side[...].reshape(2048, 128)) for side in (own_ref, other_ref)]
    for row in range(8):
        parts = [side[:, ah * 1024 + row * 128 : ah * 1024 + row * 128 + 128] for side in sides for ah in range(2)]
        largest, top = parts[0], jnp.full((8, 128), lowest, f32)
        for place, part in enumerate(parts):
            largest = jnp.maximum(largest, part)
            top = jnp.maximum(top, jnp.where(mask_ref[:, place * 128 : place * 128 + 128] > 0, part, lowest))
        top = jnp.max(top, axis=1, keepdims=True)
        top = jnp.where(top > -1e38, top, jnp.max(largest, axis=1, keepdims=True))
        for ah in range(2):
            at = ah * 16 + row % 4 * 4
            held_ref[row // 4, at : at + 4, :] = (parts[ah] - top)[0:4]
    out_ref[...] = jnp.broadcast_to(held_ref[...].astype(bf16)[None, :, None], (8, 2, 8, 32, 128))


def start_kernel(core_ref, kept_ref, own_ref, other_ref, rest_ref, mask_ref, w_in_ref, w_out_ref, pair_ref, next_ref,
                 out_ref, extra_ref, bias_ref, after_ref):
    core = core_ref[0]
    to = lax.broadcasted_iota(jnp.int32, (256, 256), 0)
    place = (to // 8 % 2 * 8 + to % 8) * 16 + (to // 16 % 4) * 4 + to // 64
    order = (lax.broadcasted_iota(jnp.int32, (256, 256), 1) == place).astype(f32).astype(bf16)
    for half in range(2):
        source = core if half == 0 else 1 - core
        mask_bias = mask_ref[:, half * 256 : half * 256 + 256]
        for block in range(4):
            taken = [
                rest_ref[block * 2 : block * 2 + 2, source, :, part * 16 : part * 16 + 16, :].reshape(256, 128)
                for part in range(2)
            ]
            placed = nn(order, jnp.concatenate(taken, axis=1)) * log2e + mask_bias
            for head in range(4):
                for part in range(4):
                    at = head * 64 + part * 16
                    bias_ref[head, part * 64 + block * 16 : part * 64 + block * 16 + 16, half * 256 : half * 256 + 256] = (
                        placed[at : at + 16]
                    )
    heads = head_lanes(256)
    ones = jnp.ones((512, 128), bf16)

    def two_rows(step, carry):
        rows = pl.ds(step * 8, 8)
        projected = nn(own_ref[:, rows].reshape(2048, 128), w_in_ref[...])
        projected_other = nn(other_ref[:, rows].reshape(2048, 128), w_in_ref[:, 128:384])
        gated = []
        for row in range(8):
            one, two = (
                jnp.concatenate([whole[row * 128 : row * 128 + 128], whole[1024 + row * 128 : 1152 + row * 128]], axis=0)
                for whole in (projected, projected_other)
            )
            query = (one[:, :128] * (32 ** (-0.5) * log2e)).astype(bf16)
            keys = jnp.concatenate([one[:, 128:256], two[:, :128]], axis=0).astype(bf16)
            values = jnp.concatenate([one[:, 256:384], two[:, 128:]], axis=0).astype(bf16)
            values = jnp.concatenate([values, ones], axis=1)
            queries = jnp.concatenate([jnp.where(lanes, query, jnp.zeros_like(query)) for lanes in heads], axis=0)
            scores = nt(queries, keys)
            attended = jnp.zeros((256, 128), f32)
            for head in range(4):
                part = scores[head * 256 : head * 256 + 256] + bias_ref[head]
                weights = jnp.exp2((part - jnp.max(part, axis=1, keepdims=True)).astype(bf16))
                summed = nn(weights, values)
                attended = jnp.where(heads[head], summed[:, :128] / summed[:, 128:], attended)
            gated.append((attended * jax.nn.sigmoid(one[:, 384:])).astype(bf16))
        update = nn(jnp.concatenate(gated, axis=0), w_out_ref[...])
        for row in range(8):
            at = step * 8 + row
            pair = pair_ref[:, at].reshape(256, 128).astype(f32)
            out_ref[:, at] = (pair + update[row * 256 : row * 256 + 256]).astype(bf16).reshape(2, 128, 128)
        return carry

    lax.fori_loop(0, 1, two_rows, 0)
    for row in range(8):
        normed = layer_norm(out_ref[:, row].reshape(256, 128).astype(f32)).astype(bf16)
        after_ref[row] = nt(next_ref[...], normed)
    largest, top = after_ref[0], jnp.full((8, 256), lowest, f32)
    for row in range(8):
        largest = jnp.maximum(largest, after_ref[row])
        top = jnp.maximum(top, jnp.where(kept_ref[row] > 0, after_ref[row], lowest))
    top = jnp.where(top > -1e38, top, largest).astype(bf16).astype(f32)
    for ah in range(2):
        extra_ref[ah, 32:40, :] = top[:, ah * 128 : ah * 128 + 128]
        for row in range(8):
            remains = after_ref[row] - top
            extra_ref[ah, row * 4 : row * 4 + 4, :] = remains[0:4, ah * 128 : ah * 128 + 128]


def end_kernel(core_ref, pieces_ref, other_ref, top_ref, mask_ref, w_in_ref, w_turned_ref, w_out_ref, out_ref, bias_ref,
               own_ref, both_ref):
    core = core_ref[0]
    to = lax.broadcasted_iota(jnp.int32, (256, 256), 0)
    key = to // 16 % 2 * 4 + to // 32 % 2 * 2 + to // 8 % 2
    place = to % 8 * 32 + key * 4 + to // 64
    order = (lax.broadcasted_iota(jnp.int32, (256, 256), 1) == place).astype(f32).astype(bf16)
    to = lax.broadcasted_iota(jnp.int32, (256, 64), 0)
    order_top = (lax.broadcasted_iota(jnp.int32, (256, 64), 1) == to % 8 * 8 + to // 64).astype(f32).astype(bf16)
    for block in range(8):
        rest = jnp.concatenate([pieces_ref[block, t, :, 16:48, :].reshape(256, 128) for t in range(2)], axis=1)
        top = jnp.concatenate([top_ref[block, t].reshape(64, 128).astype(bf16) for t in range(2)], axis=1)
        placed = (nn(order, rest) + nn(order_top, top)) * log2e
        for ah in range(2):
            half = core if ah == 0 else 1 - core
            for part in range(4):
                rows = pl.ds(pl.multiple_of(half * 256 + part * 64 + block * 8, 8), 8)
                mask_bias = mask_ref[rows, :]
                for head in range(4):
                    at = head * 64 + ah * 32 + part * 8
                    bias_ref[head, rows, :] = placed[at : at + 8] + mask_bias
    for block in range(8):
        for t in range(2):
            rows = slice(block * 128, block * 128 + 128)
            own_ref[t, rows, :] = pieces_ref[block, t, :, 0:16, :].astype(f32).reshape(128, 128)
            both_ref[t, rows, :] = other_ref[block, t].astype(f32).reshape(128, 128)
    heads = head_lanes(512)
    ones = jnp.ones((16, 512), bf16)

    def taken(from_ref, column):
        return jnp.concatenate(
            [from_ref[column // 4, pl.ds(column % 4 * 4 + part, 64, stride=16), :] for part in range(4)], axis=0
        )

    def two_columns(step, carry):
        pair = jnp.concatenate([taken(own_ref, step * 8 + place) for place in range(8)], axis=0)
        other = jnp.concatenate([taken(both_ref, step * 8 + place) for place in range(8)], axis=0)
        own, other = layer_norm(pair).astype(bf16), layer_norm(other).astype(bf16)
        first = nn(own, w_in_ref[:, :256])
        query = (first[:, :128] * (32 ** (-0.5) * log2e)).astype(bf16)
        keys_own, keys_other = first[:, 128:].astype(bf16), nn(other, w_in_ref[:, 128:256]).astype(bf16)
        turned = nt(w_turned_ref[...], own)
        values_own, values_other = turned[:128].astype(bf16), nt(w_turned_ref[:128], other).astype(bf16)
        gate = jax.nn.sigmoid(turned[128:])
        gated = []
        for place in range(8):
            at = slice(place * 256, place * 256 + 256)
            keys = jnp.concatenate([keys_own[at], keys_other[at]], axis=0)
            values = jnp.concatenate([values_own[:, at], values_other[:, at]], axis=1)
            stacked = jnp.concatenate([jnp.where(lanes, keys, jnp.zeros_like(keys)) for lanes in heads], axis=0)
            scores = nt(stacked, query[at])
            attended = []
            for head in range(4):
                part = scores[head * 512 : head * 512 + 512] + bias_ref[head]
                weights = jnp.exp2((part - jnp.max(part, axis=0, keepdims=True)).astype(bf16))
                summed = nn(jnp.concatenate([values[head * 32 : head * 32 + 32], ones], axis=0), weights)
                attended.append(summed[:32] / summed[32:33])
            gated.append(jnp.concatenate(attended, axis=0))
        gated = (jnp.concatenate(gated, axis=1) * gate).astype(bf16)
        result = (pair + dot(gated, w_out_ref[...], ((0,), (0,)))).astype(bf16)
        out_ref[pl.ds(step * 8, 8)] = result.reshape(8, 256, 128)
        return carry

    lax.fori_loop(0, 1, two_columns, 0)


def call(kernel, in_kinds, outs, scratch, flops):
    spaces = {"s": pltpu.SMEM, "v": pltpu.VMEM}
    return pl.pallas_call(
        kernel,
        out_shape=outs,
        in_specs=[pl.BlockSpec(memory_space=spaces[kind]) for kind in in_kinds],
        out_specs=jax.tree.map(lambda _: pl.BlockSpec(memory_space=pltpu.VMEM), outs),
        scratch_shapes=scratch,
        compiler_params=pltpu.CompilerParams(vmem_limit_bytes=40 * 2**20),
        cost_estimate=pl.CostEstimate(flops=flops, bytes_accessed=4 * 2**20, transcendentals=4 * 2**20),
    )


def body(pair, mask, tri_in, tri_out, start_in, start_bias, start_out, end_in, end_bias, end_out):
    q = lax.axis_index(("xl", "y"))
    core = lax.axis_index("core")
    c = lax.axis_index(("z", "xh"))
    maskf = mask.astype(f32)

    rows = swap(pair.reshape(16, 128, 128), by_row).reshape(8, 2, 2, 2, 32, 128)

    row_mask = lax.dynamic_slice_in_dim(maskf, (2 * q + core) * 32, 32)
    col_mask = lax.dynamic_slice_in_dim(maskf, c * 64, 64)
    pair_mask = (row_mask.reshape(8, 2, 2).transpose(2, 0, 1).reshape(16, 2, 1) * col_mask).reshape(8, 256)
    both = call(
        terms_kernel,
        "vvv",
        (jax.ShapeDtypeStruct((128, 16, 128), bf16),) * 2,
        [pltpu.VMEM((2, 2048, 128), f32)],
        3 * 10**8,
    )(pair, tri_in[:, :512], pair_mask)
    both = jnp.concatenate(both, axis=1)
    both, rows = lax.optimization_barrier((both, rows))
    both = swap(both, everyone).reshape(8, 2, 8, 32, 128)
    kept = lax.dynamic_index_in_dim(rows, core, 3, False)
    given = lax.ppermute(lax.dynamic_index_in_dim(rows, 1 - core, 3, False), "core", [(0, 1), (1, 0)])
    rows = jnp.stack([jnp.where(core == 0, kept, given), jnp.where(core == 0, given, kept)])
    rows = rows.reshape(2, 8, 2, 2, 8, 2, 2, 128).transpose(5, 2, 0, 3, 6, 1, 4, 7)
    pair_rows = rows.reshape(2048, 128)
    pieces = call(
        triangle_kernel,
        "v",
        jax.ShapeDtypeStruct((8, 2, 8, 16, 128), bf16),
        [pltpu.VMEM((2, 256, 512), bf16)] * 2,
        3 * 10**8,
    )(both)
    combined = swap(pieces.reshape(128, 16, 128), everyone)

    normed_rows = layer_norm(pair_rows.astype(f32)).astype(bf16)
    gate = jax.nn.sigmoid(dot(normed_rows, tri_in[:, 512:], ((1,), (0,))))
    pair_one, normed = call(
        mix_kernel,
        "vvvv",
        (jax.ShapeDtypeStruct((16, 128, 128), bf16),) * 2,
        [pltpu.VMEM((2048, 128), f32)],
        2 * 10**8,
    )(combined, pair_rows.reshape(16, 128, 128), gate.reshape(16, 128, 128), tri_out)

    other = lax.ppermute(normed, "core", [(0, 1), (1, 0)])
    halves = mask.reshape(8, 2, 8, 2, 2).transpose(1, 3, 4, 0, 2).reshape(2, 256)
    halves = jnp.concatenate([lax.dynamic_slice_in_dim(halves, place, 1) for place in (core, 1 - core)], axis=1)
    pieces = call(
        bias_kernel,
        "vvvv",
        jax.ShapeDtypeStruct((8, 2, 8, 32, 128), bf16),
        [pltpu.VMEM((2, 32, 128), f32)],
        10**8,
    )(
        normed.reshape(2, 8, 128, 128),
        other.reshape(2, 8, 128, 128),
        jnp.pad(start_bias.T, ((0, 4), (0, 0))),
        halves.astype(f32),
    )
    rest = swap(pieces.reshape(128, 32, 128), everyone).reshape(8, 2, 8, 32, 128)
    own_rows = lax.dynamic_index_in_dim(mask.reshape(8, 2, 8, 4), c, 2, False)
    own_rows = lax.dynamic_index_in_dim(own_rows, q, 0, False).reshape(8)
    here = core.astype(jnp.int32).reshape(1)
    next_bias = jnp.pad(end_bias.T, ((0, 4), (0, 0)))
    pair_two, extra = call(
        start_kernel,
        "ssvvvvvvvv",
        (jax.ShapeDtypeStruct((2, 8, 128, 128), bf16), jax.ShapeDtypeStruct((2, 40, 128), f32)),
        [pltpu.VMEM((4, 256, 512), f32), pltpu.VMEM((8, 8, 256), f32)],
        3 * 10**9,
    )(
        here,
        own_rows,
        normed.reshape(2, 8, 128, 128),
        other.reshape(2, 8, 128, 128),
        rest,
        (halves.astype(f32) - 1.0) * (1000000000.0 * log2e),
        start_in,
        start_out,
        pair_one.reshape(2, 8, 128, 128),
        next_bias,
    )

    extra = jnp.broadcast_to(extra.astype(bf16)[None, :, None], (8, 2, 8, 40, 128)).reshape(128, 40, 128)
    pieces = pair_two.reshape(2, 2, 2, 2, 2, 8, 8, 128).transpose(6, 2, 5, 0, 4, 1, 3, 7).reshape(128, 16, 128)
    pieces = swap(jnp.concatenate([pieces, extra], axis=1), everyone)
    other = lax.ppermute(pieces[:, :16], "core", [(0, 1), (1, 0)])
    top = pieces[:, 48:].astype(f32).reshape(8, 2, 8, 8, 128)

    halves = mask.reshape(8, 2, 8, 2, 2).transpose(3, 1, 4, 0, 2).reshape(2, 256)
    halves = jnp.concatenate([lax.dynamic_slice_in_dim(halves, place, 1) for place in (core, 1 - core)], axis=1)
    result = call(
        end_kernel,
        "svvvvvvv",
        jax.ShapeDtypeStruct((8, 256, 128), bf16),
        [pltpu.VMEM((4, 512, 256), f32)] + [pltpu.VMEM((2, 1024, 128), f32)] * 2,
        3 * 10**9,
    )(
        here,
        pieces.reshape(8, 2, 8, 56, 128),
        other.reshape(8, 2, 8, 16, 128),
        top,
        ((halves.astype(f32) - 1.0) * (1000000000.0 * log2e)).reshape(512, 1),
        end_in,
        end_in[:, 256:].T,
        end_out,
    )

    pieces = result.reshape(8, 2, 2, 8, 8, 128).transpose(3, 1, 2, 4, 0, 5).reshape(16, 128, 128)
    pieces = swap(pieces, same_c).reshape(8, 2, 2, 8, 2, 4, 128).transpose(3, 1, 2, 4, 0, 5, 6)
    return pieces.reshape(32, 64, 128)


def solution(mesh):
    parts = Mesh(mesh.devices.reshape(2, 4, 2, 4, 2), everyone)
    placed = P(("xl", "y", "core"), ("z", "xh"), None)
    in_specs = (placed,) + (P(),) * 9
    return jax.shard_map(body, mesh=parts, in_specs=in_specs, out_specs=placed, check_vma=False)
```
